32 devices in a mesh: slide: 2 (over y), seq: 4 (over z), head: 2 (over x), rep: 2 (over core).
Axes of the slice: x: 2, y: 2, z: 4, core: 2. Of those that a mesh axis runs over, the one named last changes fastest.
Arguments:
- tiles: bfloat16 [16384, 768], P(('slide', 'seq', 'rep')), parts along dimension 0, may hold values from -6 to 6
- labels: int32 [16384], P(('slide', 'seq', 'rep')), parts along dimension 0, may hold values from 0 to 7
- counts: int32 [16], P(('slide', 'seq', 'rep')), parts along dimension 0, may hold values from 256 to 1024, as said below
- offsets: int32 [2, 2], P(None, 'head'), may hold values from 0 to 1, as said below
- w_query: bfloat16 [768, 128], P(None, 'head'), may hold values from -0.21875 to 0.21875
- w_key: bfloat16 [768, 128], P(None, 'head'), may hold values from -0.21875 to 0.21875
- w_value: bfloat16 [768, 128], P(None, 'head'), may hold values from -0.21875 to 0.21875
- w_out: bfloat16 [128, 768], P('head'), may hold values from -2 to 2
- ln_gain: float32 [768], replicated, may hold values from 0.5 to 1.5
- w_class: bfloat16 [768, 8], replicated, may hold values from -0.875 to 0.875
Outputs:
- tile_loss: float32 [2], P('slide'), parts along dimension 0
- grad_query: float32 [1536, 128], P('slide', 'head'), parts along dimension 0
- grad_key: float32 [1536, 128], P('slide', 'head'), parts along dimension 0
- grad_value: float32 [1536, 128], P('slide', 'head'), parts along dimension 0
- grad_out: float32 [128, 1536], P('head', 'slide'), parts along dimension 1
The draws below stay inside these ranges and needn't reach their ends.
There are 2 independent parts, one for each index of `slide`. The reference program is written for one: setup_inputs(seed, part) draws one part's arguments, and reference() takes and returns one part's arrays. A program takes and returns all parts, laid end to end along the dimension named above; an argument that names none is the same for every part. Nothing has to cross between parts.
Inputs may be any that keep to these rules, and one draw needn't show every extreme that they name: `counts`: valid tiles of each device's slots; some device of every slide holds 1024. `offsets`: row 0 is below 2 and takes every value below it over the heads; row 1 is distinct over the heads.
All inputs are finite; a program needn't handle non-finite values.
Results may differ from the reference program's by a relative error of at most 0.017.
Values may be sent and summed in bfloat16 or wider, within the bound.
A program may use at most 128 MiB of HBM per device.

```python
import math
import jax
import jax.numpy as jnp
from jax import lax

D = 768
HD = 64
CLASSES = 8
TOK_DEV = 1024
HEAD_TOTAL = 2
TILE_DEVICES = 8
DILATION_THIRD = 2
TOKENS = 8192
N_REP = 2


def draw_counts(key, part):
    key = jax.random.fold_in(key, 11)
    first, second_rate = jax.random.split(key)
    drawn = jax.random.randint(first, (TILE_DEVICES,), TOK_DEV // 4, TOK_DEV + 1)
    fullest = jax.random.randint(second_rate, (), 0, TILE_DEVICES)
    return jnp.where(jnp.arange(TILE_DEVICES) == fullest, TOK_DEV, drawn).astype(jnp.int32)


def draw_offsets(key, part):
    key = jax.random.fold_in(key, 23)
    first, second_rate = jax.random.split(key)
    paired = jax.random.permutation(first, HEAD_TOTAL) % N_REP
    spaced_rows = jax.random.permutation(second_rate, DILATION_THIRD)[:HEAD_TOTAL]
    return jnp.stack([paired, spaced_rows], axis=0).astype(jnp.int32)


def plant(values, key, smallest, high):
    shape = values.shape
    spot = [jax.random.randint(jax.random.fold_in(key, axis), (), 0, shape[axis]) for axis in range(len(shape))]
    values = values.at[tuple(spot)].set(smallest)
    longest = shape.index(max(shape))
    spot[longest] = (spot[longest] + 1) % shape[longest]
    return values.at[tuple(spot)].set(high)


def levels(key, extent, cuts, smallest, high):
    level, own = 1.0, jax.random.fold_in(key, 6)
    for dim, blocks in cuts:
        heights = jnp.exp(jax.random.uniform(jax.random.fold_in(own, dim), (blocks,), jnp.float32, smallest / len(cuts), high / len(cuts)))
        level = level * jnp.repeat(heights, extent[dim] // blocks).reshape([-1 if axis == dim else 1 for axis in range(len(extent))])
    return level


def noise(key, dims, width, most, pieces=(), kind=jnp.bfloat16):
    array = jax.random.normal(key, dims, jnp.float32) * width
    if len(pieces) > 0:
        array = levels(key, dims, pieces, -0.22, 0.18) * array
    return jnp.clip(array, min=-most, max=most).astype(kind)


def setup_inputs(seed: int = 0, part: int = 0) -> dict:
    arg_keys = jax.random.split(jax.random.key(seed), 11)
    part_keys = jax.random.split(jax.random.fold_in(arg_keys[10], part), 11)
    tiles = noise(part_keys[0], (TOKENS, D), 1.0, 6.0, ((0, 8),))
    labels = plant(jax.random.randint(part_keys[1], (TOKENS,), 0, CLASSES), jax.random.fold_in(part_keys[1], 1), 0, CLASSES - 1).astype(jnp.int32)
    counts = draw_counts(jax.random.fold_in(jax.random.fold_in(arg_keys[10], part), 71), part)
    offsets = draw_offsets(jax.random.fold_in(arg_keys[10], 71), part)
    w_query = noise(arg_keys[4], (D, HEAD_TOTAL * HD), D ** -0.5, 0.21875, ((1, 2),))
    w_key = noise(arg_keys[5], (D, HEAD_TOTAL * HD), D ** -0.5, 0.21875, ((1, 2),))
    w_value = noise(arg_keys[6], (D, HEAD_TOTAL * HD), D ** -0.5, 0.21875, ((1, 2),))
    w_out = noise(arg_keys[7], (HEAD_TOTAL * HD, D), (HD // 8) ** -0.5, 2.0, ((0, 2),))
    ln_gain = jnp.clip(1.0 + 0.1 * jax.random.normal(arg_keys[8], (D,), jnp.float32), 0.5, 1.5)
    w_class = noise(arg_keys[9], (D, CLASSES), (D // 16) ** -0.5, 0.875)
    return dict(tiles=tiles, labels=labels, counts=counts, offsets=offsets, w_query=w_query, w_key=w_key, w_value=w_value, w_out=w_out, ln_gain=ln_gain, w_class=w_class)


def layout(partner_offset, distant_offset):
    return ((TILE_DEVICES, 1, 0), (TILE_DEVICES // N_REP, N_REP, partner_offset), (1, DILATION_THIRD, distant_offset))

def view(source, groups, stride, offset):
    shaped = source.reshape((groups, TOKENS // (groups * stride), stride) + source.shape[1:])
    return lax.dynamic_index_in_dim(shaped, offset, axis=2, keepdims=False)

def place(values, offset, stride, filler):
    chosen = (jnp.arange(stride) == offset).reshape((1, 1, stride) + (1,) * (values.ndim - 2))
    placed = jnp.where(chosen, jnp.expand_dims(values, 2), filler)
    return placed.reshape((TOKENS,) + values.shape[2:])

def scores_of(queries, keys, key_ok):
    factor = 1.0 / math.sqrt(HD)
    raw = jnp.einsum('gnd,gmd->gnm', queries.astype(jnp.float32), keys.astype(jnp.float32)) * factor
    return jnp.where(key_ok[:, None, :], raw, -jnp.inf)

def head_forward(queries, keys, values, tile_ok, partner_offset, distant_offset):
    row_top = jnp.full((TOKENS,), -jnp.inf, jnp.float32)
    scores = []
    for groups, stride, offset in layout(partner_offset, distant_offset):
        block = scores_of(view(queries, groups, stride, offset), view(keys, groups, stride, offset), view(tile_ok, groups, stride, offset))
        scores.append(block)
        row_top = jnp.maximum(row_top, place(lax.optimization_barrier(jnp.max(block, axis=-1)), offset, stride, -jnp.inf))
    row_total = jnp.zeros((TOKENS,), jnp.float32)
    weighted = jnp.zeros((TOKENS, HD), jnp.float32)
    for member, block in zip(layout(partner_offset, distant_offset), scores):
        groups, stride, offset = member
        expo = jnp.exp(block - view(row_top, groups, stride, offset)[..., None])
        row_total = row_total + place(lax.optimization_barrier(jnp.sum(expo, axis=-1)), offset, stride, 0.0)
        summed = jnp.einsum('gnm,gmd->gnd', expo.astype(jnp.bfloat16).astype(jnp.float32), view(values, groups, stride, offset).astype(jnp.float32))
        weighted = weighted + place(summed, offset, stride, 0.0)
    return ((weighted / row_total[:, None]).astype(jnp.bfloat16), row_top, row_total)

def head_backward(queries, keys, values, tile_ok, partner_offset, distant_offset, row_top, row_total, grad_rows, delta):
    factor = 1.0 / math.sqrt(HD)
    grad_q = jnp.zeros((TOKENS, HD), jnp.float32)
    grad_k = jnp.zeros((TOKENS, HD), jnp.float32)
    grad_v = jnp.zeros((TOKENS, HD), jnp.float32)
    for groups, stride, offset in layout(partner_offset, distant_offset):
        sub_query = view(queries, groups, stride, offset).astype(jnp.float32)
        sub_key = view(keys, groups, stride, offset).astype(jnp.float32)
        sub_value = view(values, groups, stride, offset).astype(jnp.float32)
        sub_grad = view(grad_rows, groups, stride, offset).astype(jnp.float32)
        block = scores_of(view(queries, groups, stride, offset), view(keys, groups, stride, offset), view(tile_ok, groups, stride, offset))
        prob = jnp.exp(block - view(row_top, groups, stride, offset)[..., None]) / view(row_total, groups, stride, offset)[..., None]
        dprob = jnp.einsum('gnd,gmd->gnm', sub_grad, sub_value)
        dscore = (prob * (dprob - view(delta, groups, stride, offset)[..., None])).astype(jnp.bfloat16).astype(jnp.float32)
        grad_q = grad_q + place(jnp.einsum('gnm,gmd->gnd', dscore, sub_key) * factor, offset, stride, 0.0)
        grad_k = grad_k + place(jnp.einsum('gnm,gnd->gmd', dscore, sub_query) * factor, offset, stride, 0.0)
        prob_low = prob.astype(jnp.bfloat16).astype(jnp.float32)
        grad_v = grad_v + place(jnp.einsum('gnm,gnd->gmd', prob_low, sub_grad), offset, stride, 0.0)
    return (grad_q.astype(jnp.bfloat16), grad_k.astype(jnp.bfloat16), grad_v.astype(jnp.bfloat16))

def split_heads(matrix):
    return matrix.reshape(TOKENS, HEAD_TOTAL, HD).transpose(1, 0, 2)

def join_heads(stacked):
    return stacked.transpose(1, 0, 2).reshape(TOKENS, HEAD_TOTAL * HD)

def reference(tiles, labels, counts, offsets, w_query, w_key, w_value, w_out, ln_gain, w_class):
    position = jnp.arange(TOKENS, dtype=jnp.int32)
    tile_ok = position % TOK_DEV < jnp.repeat(counts, TOK_DEV)
    queries = jnp.dot(tiles, w_query, preferred_element_type=jnp.float32).astype(jnp.bfloat16)
    keys = jnp.dot(tiles, w_key, preferred_element_type=jnp.float32).astype(jnp.bfloat16)
    values = jnp.dot(tiles, w_value, preferred_element_type=jnp.float32).astype(jnp.bfloat16)
    head_offsets = offsets.T
    per_head = (split_heads(queries), split_heads(keys), split_heads(values), head_offsets)
    attended, row_top, row_total = lax.map(lambda item: head_forward(item[0], item[1], item[2], tile_ok, item[3][0], item[3][1]), per_head)

    def add_head(running, item):
        term = jnp.dot(item[0], item[1], preferred_element_type=jnp.float32).astype(jnp.bfloat16)
        return (running + term.astype(jnp.float32), None)
    projected, _ = lax.scan(add_head, jnp.zeros((TOKENS, D), jnp.float32), (attended, w_out.reshape(HEAD_TOTAL, HD, D)))
    mixed = tiles.astype(jnp.float32) + projected
    center = mixed - lax.optimization_barrier(jnp.mean(mixed, axis=-1, keepdims=True))
    inv_dev = lax.rsqrt(lax.optimization_barrier(jnp.mean(center * center, axis=-1, keepdims=True)) + 1e-05)
    normal = center * inv_dev
    normed = (normal * ln_gain).astype(jnp.bfloat16)
    logits = jnp.dot(normed, w_class, preferred_element_type=jnp.float32)
    peak = lax.optimization_barrier(jnp.max(logits, axis=-1, keepdims=True))
    log_total = jnp.log(lax.optimization_barrier(jnp.sum(jnp.exp(logits - peak), axis=-1, keepdims=True))) + peak
    onehot = (labels[:, None] == jnp.arange(CLASSES, dtype=jnp.int32)[None, :]).astype(jnp.float32)
    cross = log_total[:, 0] - lax.optimization_barrier(jnp.sum(onehot * logits, axis=-1))
    tile_loss = (jnp.sum(jnp.where(tile_ok, cross, 0.0)) / TOK_DEV).reshape(1)
    grad_logits = (jnp.exp(logits - log_total) - onehot) * tile_ok[:, None].astype(jnp.float32) / TOK_DEV
    grad_normed = jnp.dot(grad_logits, w_class.astype(jnp.float32).T, precision=lax.Precision.HIGHEST)
    grad_normal = grad_normed * ln_gain
    grad_mixed = inv_dev * (grad_normal - lax.optimization_barrier(jnp.mean(grad_normal, axis=-1, keepdims=True)) - normal * lax.optimization_barrier(jnp.mean(grad_normal * normal, axis=-1, keepdims=True)))
    grad_mixed = grad_mixed.astype(jnp.bfloat16)
    attended_all = join_heads(attended)
    grad_out = jnp.dot(attended_all.T, grad_mixed, preferred_element_type=jnp.float32)
    grad_attended = jnp.dot(grad_mixed, w_out.T, preferred_element_type=jnp.float32).astype(jnp.bfloat16)
    grad_split = split_heads(grad_attended)
    delta = lax.optimization_barrier(jnp.sum(grad_split.astype(jnp.float32) * attended.astype(jnp.float32), axis=-1))
    back_in = per_head + (row_top, row_total, grad_split, delta)
    grad_q, grad_k, grad_v = lax.map(lambda item: head_backward(item[0], item[1], item[2], tile_ok, item[3][0], item[3][1], item[4], item[5], item[6], item[7]), back_in)
    grad_query = jnp.dot(tiles.T, join_heads(grad_q), preferred_element_type=jnp.float32)
    grad_key = jnp.dot(tiles.T, join_heads(grad_k), preferred_element_type=jnp.float32)
    grad_value = jnp.dot(tiles.T, join_heads(grad_v), preferred_element_type=jnp.float32)
    return (tile_loss, grad_query, grad_key, grad_value, grad_out)
```

```python
import functools
import math

import jax
import jax.numpy as jnp
from jax import lax
from jax.experimental import pallas as pl
from jax.experimental.pallas import tpu as pltpu
from jax.sharding import PartitionSpec as P

MESH = pl.DeviceIdType.MESH
F32, BF16 = jnp.float32, jnp.bfloat16
LOW = -1e30
PERM = 256
TAIL = 16


def nn(a, b):
    return jnp.dot(a, b, preferred_element_type=F32)


def nt(a, b):
    return lax.dot_general(a, b, (((1,), (1,)), ((), ())), preferred_element_type=F32)


def tn(a, b):
    return lax.dot_general(a, b, (((0,), (0,)), ((), ())), preferred_element_type=F32)


def lanes(rows):
    return lax.broadcasted_iota(jnp.int32, (rows, 128), 1)


def subs(rows):
    return lax.broadcasted_iota(jnp.int32, (rows, 128), 0)


def three(x):
    hi = x.astype(BF16).astype(F32)
    rest = x - hi
    mid = rest.astype(BF16).astype(F32)
    return hi, mid, rest - mid


def kernel(
    dims,
    tiles, labels, counts, offsets, wqkv, w_out, gain, wcc,
    res, loss_out,
    xt, qs, kvs, ka0, va0, kv_all, ka2, va2, pr, ka1, va1, att_pk, wo,
    acc0, m0, acc1, m1, qa, doa, atb, dmix, dq, dqp, dkv, dkvp,
    rs_out, rs_sib, rs_mid, rs_z, pr_out, pr_in, lt, ltz,
    pan, pan_sib, pan_half, pan_z,
    s_far, r_far, s_fwd, r_fwd, s_pr, r_pr, s_w, r_w, s_att, r_att,
    s_rs, r_rs, s_rz, r_rz, s_pb, r_pb, s_l, r_l, s_lz, r_lz,
    s_a1, r_a1, s_a2, r_a2, s_a3, r_a3, s_a4, r_a4,
):
    ns, nh, ps, fs, hs, classes, piece = dims
    n, d = tiles.shape
    far, half = n // fs, n // ps
    sub_count = fs // ps
    z, h, p = lax.axis_index("seq"), lax.axis_index("head"), lax.axis_index("rep")

    def at_z(dz):
        return {"seq": lax.rem(z + dz, ns)}

    def at_p(dp):
        return {"rep": lax.rem(p + dp, ps)}

    def at_h(dh):
        return {"head": lax.rem(h + dh, nh)}

    sends = []

    def push(src, dst, ssem, rsem, where):
        copy = pltpu.make_async_remote_copy(
            src_ref=src, dst_ref=dst, send_sem=ssem, recv_sem=rsem,
            device_id=where, device_id_type=MESH,
        )
        copy.start()
        sends.append(copy)
        return copy

    barrier = pltpu.get_barrier_semaphore()
    peers = (
        [at_z(i) for i in range(1, ns)]
        + [at_p(i) for i in range(1, ps)]
        + [at_h(i) for i in range(1, nh)]
    )
    for peer in peers:
        pl.semaphore_signal(barrier, inc=1, device_id=peer, device_id_type=MESH)

    residues = [(c % sub_count) * ps + c // sub_count for c in range(fs)]
    count = counts[0]
    o1 = offsets[0, 0]
    o2 = offsets[1, 0]
    c2 = lax.rem(o2, ps) * sub_count + lax.div(o2, ps)

    def rows_of(c):
        return pl.ds(c * far, far)

    per = PERM // fs
    a = lax.broadcasted_iota(jnp.int32, (PERM, PERM), 0)
    b = lax.broadcasted_iota(jnp.int32, (PERM, PERM), 1)
    want = jnp.zeros((PERM, PERM), jnp.int32)
    for c in range(fs):
        want = jnp.where((a >= c * per) & (a < (c + 1) * per), (a - c * per) * fs + residues[c], want)
    perm = (want == b).astype(F32).astype(BF16)
    for blk in range(n // PERM):
        moved = nn(perm, tiles[pl.ds(blk * PERM, PERM), :]).astype(BF16)
        qkv = nn(moved, wqkv[...])
        q_part = (qkv[:, :128] * (1.0 / math.sqrt(hs))).astype(BF16)
        kv_part = qkv[:, 128:].astype(BF16)
        for c in range(fs):
            spot = pl.ds(c * far + blk * per, per)
            xt[spot, :] = moved[c * per:(c + 1) * per, :]
            qs[spot, :] = q_part[c * per:(c + 1) * per, :]
            kvs[spot, :] = kv_part[c * per:(c + 1) * per, :]

    def pick_far(ref):
        out = ref[rows_of(0), :].astype(F32)
        for c in range(1, fs):
            out = jnp.where(c2 == c, ref[rows_of(c), :].astype(F32), out)
        return out

    def pick_half(ref):
        out = ref[pl.ds(0, half), :].astype(F32)
        for c in range(1, ps):
            out = jnp.where(o1 == c, ref[pl.ds(c * half, half), :].astype(F32), out)
        return out

    high = lax.div(count, 256)
    tail = jnp.where(subs(TAIL) < 8, high.astype(F32), (count - high * 256).astype(F32)).astype(BF16)
    kv_all[0, 0, pl.ds(0, far), :] = pick_far(kvs).astype(BF16)
    kv_all[0, 0, pl.ds(far, TAIL), :] = tail
    pr[0, pl.ds(0, half), :] = pick_half(kvs).astype(BF16)
    pr[0, pl.ds(half, TAIL), :] = tail

    wo[:, pl.ds(0, hs), :] = jnp.zeros((nh, hs, d), BF16)
    wo[:, pl.ds(2 * hs, hs), :] = jnp.zeros((nh, hs, d), BF16)
    wo[0, pl.ds(hs, hs), :] = w_out[...]

    pl.semaphore_wait(barrier, len(peers))
    far_z = {}
    for dz in range(1, ns):
        far_z[dz] = push(kv_all.at[0, 0], kv_all.at[dz, 0], s_far.at[dz], r_far.at[dz], at_z(dz))
    pr_c, fwd_c, w_c, att_c = {}, {}, {}, {}
    for dp in range(1, ps):
        pr_c[dp] = push(pr.at[0], pr.at[dp], s_pr.at[dp], r_pr.at[dp], at_p(dp))
        fwd_c[0, dp] = push(kv_all.at[0, 0], kv_all.at[0, dp], s_fwd.at[0, dp], r_fwd.at[0, dp], at_p(dp))
    for dh in range(1, nh):
        w_c[dh] = push(
            wo.at[0, pl.ds(hs, hs), :], wo.at[dh, pl.ds(hs, hs), :], s_w.at[dh], r_w.at[dh], at_h(dh)
        )

    def augment(kv, original, cnt):
        rows = kv.shape[0]
        lane = lanes(rows)
        kv = kv.astype(F32)
        bias = jnp.where(original.astype(F32) < cnt, 0.0, LOW)
        key = jnp.where(lane < hs, kv, jnp.where(lane == hs, bias, 1.0))
        value = jnp.where(lane < hs, 1.0, kv)
        return key.astype(BF16), value.astype(BF16)

    def remote_count(tail):
        tail = tail.astype(F32)
        return tail[0:1, 0:1] * 256.0 + tail[8:9, 0:1]

    def with_one(q):
        return jnp.where(lanes(q.shape[0]) == hs, 1.0, q.astype(F32)).astype(BF16)

    def forward(q, key, value):
        s = nt(q, key)
        top = jnp.max(s, axis=-1, keepdims=True)
        return top, nn(jnp.exp(s - top).astype(BF16), value)

    own_count = count.astype(F32)
    step = min(256, far)
    for c in range(fs):
        key, value = augment(kvs[rows_of(c), :], subs(far) * fs + residues[c], own_count)
        ka0[rows_of(c), :] = key
        va0[rows_of(c), :] = value
    wide = min(256, n)
    for i in range(n // wide):
        spot = pl.ds(i * wide, wide)
        top, acc = forward(with_one(qs[spot, :]), ka0[...], va0[...])
        m0[spot, :] = jnp.broadcast_to(top, (wide, 128))
        acc0[spot, :] = acc
    for dp in range(ps):
        if dp:
            pr_c[dp].wait_recv()
        cnt = remote_count(pr[dp, pl.ds(half, TAIL), :])
        for k in range(sub_count):
            key, value = augment(pr[dp, pl.ds(k * far, far), :], subs(far) * fs + k * ps + o1, cnt)
            ka1[pl.ds(dp * half + k * far, far), :] = key
            va1[pl.ds(dp * half + k * far, far), :] = value
    q_half = with_one(pick_half(qs))
    wide = min(256, half)
    for i in range(half // wide):
        spot = pl.ds(i * wide, wide)
        top, acc = forward(q_half[i * wide:(i + 1) * wide, :], ka1[...], va1[...])
        m1[spot, :] = jnp.broadcast_to(top, (wide, 128))
        acc1[spot, :] = acc

    q_far = with_one(pick_far(qs))
    order = [(0, dp) for dp in range(ps)]
    for dz in range(1, ns):
        order += [(dz, dp) for dp in range(ps)]
    top2 = acc2 = None
    for dz in range(1, ns):
        far_z[dz].wait_recv()
        for dp in range(1, ps):
            fwd_c[dz, dp] = push(
                kv_all.at[dz, 0], kv_all.at[dz, dp], s_fwd.at[dz, dp], r_fwd.at[dz, dp], at_p(dp)
            )
        for bz, dp in [(dz - 1, i) for i in range(ps)] + ([(dz, i) for i in range(ps)] if dz == ns - 1 else []):
            if dp:
                fwd_c[bz, dp].wait_recv()
            key, value = augment(
                kv_all[bz, dp, pl.ds(0, far), :], subs(far) * fs + o2,
                remote_count(kv_all[bz, dp, pl.ds(far, TAIL), :]),
            )
            ka2[bz * ps + dp] = key
            va2[bz * ps + dp] = value
            top, acc = forward(q_far, key, value)
            if top2 is None:
                top2, acc2 = top, acc
            else:
                both = jnp.maximum(top, top2)
                acc2 = acc2 * jnp.exp(top2 - both) + acc * jnp.exp(top - both)
                top2 = both

    for c in range(fs):
        rows = rows_of(c)
        in_half = pl.ds((c % sub_count) * far, far)
        t0 = m0[rows, 0:1]
        t1 = jnp.where(o1 == c // sub_count, m1[in_half, 0:1], LOW)
        t2 = jnp.where(c2 == c, top2, LOW)
        top = jnp.maximum(t0, jnp.maximum(t1, t2))
        acc = acc0[rows, :] * jnp.exp(t0 - top) + acc1[in_half, :] * jnp.exp(t1 - top) + acc2 * jnp.exp(t2 - top)
        total = acc[:, 0:1]
        lane = lanes(far)
        att = jnp.where(lane < hs, 0.0, acc / total)
        atb[rows, :] = att.astype(BF16)
        one, two, rest = three(-(top + jnp.log(total)))
        aux = jnp.where(lane == hs, 1.0, jnp.where(lane == hs + 1, one, jnp.where(lane == hs + 2, two, jnp.where(lane == hs + 3, rest, 0.0))))
        qa[rows, :] = jnp.where(lane < hs, qs[rows, :].astype(F32), aux).astype(BF16)
    mid = n // 2
    att_pk[0, :, :] = (
        atb[pl.ds(0, mid), :].astype(F32) + pltpu.roll(atb[pl.ds(mid, mid), :].astype(F32), hs, 1)
    ).astype(BF16)
    for dh in range(1, nh):
        att_c[dh] = push(att_pk.at[0], att_pk.at[dh], s_att.at[dh], r_att.at[dh], at_h(dh))
    for dh in range(1, nh):
        w_c[dh].wait_recv()
    for dh in range(1, nh):
        att_c[dh].wait_recv()

    loss = jnp.zeros((1, 1), F32)
    g = gain[...]
    for i in range(n // step):
        start = i * step
        c, inner = start // far, start % far
        rows = pl.ds(start, step)
        mixed = xt[rows, :].astype(F32)
        for dh in range(nh):
            if start < mid:
                term = nn(att_pk[dh, pl.ds(start, step), :], wo[dh, pl.ds(0, 2 * hs), :])
            else:
                term = nn(att_pk[dh, pl.ds(start - mid, step), :], wo[dh, pl.ds(hs, 2 * hs), :])
            mixed = mixed + term.astype(BF16).astype(F32)
        center = mixed - jnp.mean(mixed, axis=-1, keepdims=True)
        inv_dev = lax.rsqrt(jnp.mean(center * center, axis=-1, keepdims=True) + 1e-05)
        normal = center * inv_dev
        normed = (normal * g).astype(BF16)
        logits = nt(wcc[...], normed)[:classes, :]
        peak = jnp.max(logits, axis=0, keepdims=True)
        log_total = jnp.log(jnp.sum(jnp.exp(logits - peak), axis=0, keepdims=True)) + peak
        kind = lax.broadcasted_iota(jnp.int32, (classes, step), 0)
        onehot = (kind == labels[:, pl.ds(start, step)]).astype(F32)
        spot = lax.broadcasted_iota(jnp.int32, (1, step), 1)
        ok = ((spot + inner) * fs + residues[c] < count).astype(F32)
        cross = log_total - jnp.sum(onehot * logits, axis=0, keepdims=True)
        loss = loss + jnp.sum(ok * cross, axis=1, keepdims=True)
        d_logits = (jnp.exp(logits - log_total) - onehot) * ok * (1.0 / n)
        hi = d_logits.astype(BF16).astype(F32)
        split = jnp.concatenate([hi, d_logits - hi], axis=0).astype(BF16)
        d_normal = tn(split, wcc[...]) * g
        d_mixed = inv_dev * (
            d_normal
            - jnp.mean(d_normal, axis=-1, keepdims=True)
            - normal * jnp.mean(d_normal * normal, axis=-1, keepdims=True)
        )
        d_mixed = d_mixed.astype(BF16)
        dmix[rows, :] = d_mixed
        d_att = nt(d_mixed, wo[0, pl.ds(0, 2 * hs), :]).astype(BF16).astype(F32)
        delta = jnp.sum(d_att * atb[rows, :].astype(F32), axis=-1, keepdims=True)
        one, two, rest = three(-delta)
        lane = lanes(step)
        aux = jnp.where(lane == 0, one, jnp.where(lane == 1, two, jnp.where(lane == 2, rest, d_att)))
        doa[rows, :] = aux.astype(BF16)
    lt[0, :, :] = jnp.broadcast_to(loss * (1.0 / n), (8, 128))
    lt_c = {dp: push(lt.at[0], lt.at[dp], s_l.at[dp], r_l.at[dp], at_p(dp)) for dp in range(1, ps)}

    def backward(q, do, key, value):
        prob = jnp.exp(nt(key, q))
        d_score = (prob * nt(value, do)).astype(BF16)
        d_key = nn(d_score, q)
        d_value = nn(prob.astype(BF16), do)
        return tn(d_score, key), jnp.where(lanes(key.shape[0]) < hs, d_key, d_value)

    q_far = pick_far(qa).astype(BF16)
    do_far = pick_far(doa).astype(BF16)
    dq_far = None
    rz_c = {}
    own_far = None
    for dz in list(range(1, ns)) + [0]:
        rs_c = {}
        own = None
        for dp in list(range(1, ps)) + [0]:
            key_rows = dz * ps + dp
            d_q, d_kv = backward(q_far, do_far, ka2[key_rows], va2[key_rows])
            dq_far = d_q if dq_far is None else dq_far + d_q
            if dp:
                rs_out[dz, dp] = d_kv.astype(BF16)
                rs_c[dp] = push(
                    rs_out.at[dz, dp], rs_sib.at[dz, dp], s_rs.at[dz, dp], r_rs.at[dz, dp], at_p(ps - dp)
                )
            else:
                own = d_kv
        for dp in range(1, ps):
            rs_c[dp].wait_recv()
            own = own + rs_sib[dz, dp].astype(F32)
        if dz:
            rs_mid[dz] = own.astype(BF16)
            rz_c[dz] = push(rs_mid.at[dz], rs_z.at[dz], s_rz.at[dz], r_rz.at[dz], at_z(ns - dz))
        else:
            own_far = own

    whole_loss = lt[0, :, :]
    for dp in range(1, ps):
        lt_c[dp].wait_recv()
        whole_loss = whole_loss + lt[dp, :, :]
    ltz[0, :, :] = whole_loss
    lz_c = {dz: push(ltz.at[0], ltz.at[dz], s_lz.at[dz], r_lz.at[dz], at_z(dz)) for dz in range(1, ns)}

    q_half = pick_half(qa).astype(BF16)
    do_half = pick_half(doa).astype(BF16)
    pb_c = {}
    dq_half = None
    for dp in list(range(1, ps)) + [0]:
        key_rows = pl.ds(dp * half, half)
        d_q, d_kv = backward(q_half, do_half, ka1[key_rows, :], va1[key_rows, :])
        dq_half = d_q if dq_half is None else dq_half + d_q
        if dp:
            pr_out[dp] = d_kv.astype(BF16)
            pb_c[dp] = push(pr_out.at[dp], pr_in.at[dp], s_pb.at[dp], r_pb.at[dp], at_p(ps - dp))
        else:
            dkvp[...] = d_kv
    dqp[...] = dq_half

    tile = min(512, n)
    for j in range(n // tile):
        key_rows = pl.ds(j * tile, tile)
        total = None
        for i in range(n // tile):
            rows = pl.ds(i * tile, tile)
            d_q, d_kv = backward(qa[rows, :], doa[rows, :], ka0[key_rows, :], va0[key_rows, :])
            total = d_kv if total is None else total + d_kv
            if j:
                dq[rows, :] += d_q
            else:
                dq[rows, :] = d_q
        dkv[key_rows, :] = total

    for c in range(fs):
        rows = rows_of(c)
        in_half = pl.ds((c % sub_count) * far, far)
        part = dq[rows, :]
        part = part + jnp.where(o1 == c // sub_count, dqp[in_half, :], 0.0)
        part = part + jnp.where(c2 == c, dq_far, 0.0)
        qa[rows, :] = jnp.where(lanes(far) < hs, part * (1.0 / math.sqrt(hs)), 0.0).astype(BF16)

    quarter = ns * piece
    first, second, third, fourth = {}, {}, {}, {}

    def start_panel(k, panel):
        pan[k, pl.ds(0, d), :] = panel.astype(BF16)
        if quarter * ps > d:
            pan[k, pl.ds(d, quarter * ps - d), :] = jnp.zeros((quarter * ps - d, 128), BF16)
        for dp in range(1, ps):
            there = pl.multiple_of(lax.rem(p + dp, ps) * quarter, 16)
            first[k, dp] = push(
                pan.at[k, pl.ds(there, quarter), :], pan_sib.at[k, dp],
                s_a1.at[k, dp], r_a1.at[k, dp], at_p(dp),
            )

    def second_panel(k):
        here = pl.multiple_of(p * quarter, 16)
        total = pan[k, pl.ds(here, quarter), :].astype(F32)
        for dp in range(1, ps):
            first[k, dp].wait_recv()
            total = total + pan_sib[k, dp].astype(F32)
        pan_half[k] = total.astype(BF16)
        for dz in range(1, ns):
            there = pl.multiple_of(lax.rem(z + dz, ns) * piece, 16)
            second[k, dz] = push(
                pan_half.at[k, pl.ds(there, piece), :], pan_z.at[k, dz],
                s_a2.at[k, dz], r_a2.at[k, dz], at_z(dz),
            )

    def third_panel(k):
        here = pl.multiple_of(z * piece, 16)
        total = pan_half[k, pl.ds(here, piece), :].astype(F32)
        for dz in range(1, ns):
            second[k, dz].wait_recv()
            total = total + pan_z[k, dz].astype(F32)
        spot = pl.ds(pl.multiple_of(p * quarter + z * piece, 16), piece)
        res[k, spot, :] = total.astype(BF16)
        for dz in range(1, ns):
            third[k, dz] = push(
                res.at[k, spot, :], res.at[k, spot, :], s_a3.at[k, dz], r_a3.at[k, dz], at_z(dz)
            )

    def fourth_panel(k):
        for dz in range(1, ns):
            third[k, dz].wait_recv()
        spot = pl.ds(pl.multiple_of(p * quarter, 16), quarter)
        for dp in range(1, ps):
            fourth[k, dp] = push(
                res.at[k, spot, :], res.at[k, spot, :], s_a4.at[k, dp], r_a4.at[k, dp], at_p(dp)
            )

    start_panel(0, tn(xt[...], qa[...]) + tn(dmix[...], atb[...]))

    half_sum = dkvp[...]
    for dp in range(1, ps):
        pb_c[dp].wait_recv()
        half_sum = half_sum + pr_in[dp].astype(F32)
    dkvp[...] = half_sum
    for dz in range(1, ns):
        rz_c[dz].wait_recv()
        own_far = own_far + rs_z[dz].astype(F32)
    for c in range(fs):
        rows = rows_of(c)
        in_half = pl.ds((c % sub_count) * far, far)
        part = dkv[rows, :]
        part = part + jnp.where(o1 == c // sub_count, dkvp[in_half, :], 0.0)
        part = part + jnp.where(c2 == c, own_far, 0.0)
        doa[rows, :] = part.astype(BF16)
    second_panel(0)
    start_panel(1, tn(xt[...], doa[...]))
    third_panel(0)
    second_panel(1)
    fourth_panel(0)
    third_panel(1)
    total = ltz[0, :, :]
    for dz in range(1, ns):
        lz_c[dz].wait_recv()
        total = total + ltz[dz, :, :]
    loss_out[...] = total
    fourth_panel(1)
    for k in range(2):
        for dp in range(1, ps):
            fourth[k, dp].wait_recv()
    for copy in sends:
        copy.wait_send()


def body(ns, nh, ps, tiles, labels, counts, offsets, w_query, w_key, w_value, w_out, ln_gain, w_class):
    n, d = tiles.shape
    hs = w_query.shape[1]
    classes = w_class.shape[1]
    shards = ns * ps
    fs = shards // 4
    far, half = n // fs, n // ps
    piece = -(-d // (shards * 16)) * 16
    quarter = ns * piece
    labels_row = labels.reshape(far, fs // ps, ps).transpose(2, 1, 0).reshape(1, n)
    wqkv = jnp.concatenate([w_query, jnp.zeros((d, 128 - hs), BF16), w_key, w_value], axis=1)
    wcc = jnp.concatenate([w_class.T, w_class.T], axis=0)
    vmem = pltpu.VMEM
    dma = lambda *shape: pltpu.SemaphoreType.DMA(shape)
    scratch = [
        vmem((n, d), BF16), vmem((n, 128), BF16), vmem((n, 128), BF16),
        vmem((n, 128), BF16), vmem((n, 128), BF16),
        vmem((ns, ps, far + TAIL, 128), BF16),
        vmem((shards, far, 128), BF16), vmem((shards, far, 128), BF16),
        vmem((ps, half + TAIL, 128), BF16), vmem((n, 128), BF16), vmem((n, 128), BF16),
        vmem((nh, n // 2, 128), BF16), vmem((nh, 3 * hs, d), BF16),
        vmem((n, 128), F32), vmem((n, 128), F32), vmem((half, 128), F32), vmem((half, 128), F32),
        vmem((n, 128), BF16), vmem((n, 128), BF16), vmem((n, 128), BF16), vmem((n, d), BF16),
        vmem((n, 128), F32), vmem((half, 128), F32), vmem((n, 128), F32), vmem((half, 128), F32),
        vmem((ns, ps, far, 128), BF16), vmem((ns, ps, far, 128), BF16),
        vmem((ns, far, 128), BF16), vmem((ns, far, 128), BF16),
        vmem((ps, half, 128), BF16), vmem((ps, half, 128), BF16),
        vmem((ps, 8, 128), F32), vmem((ns, 8, 128), F32),
        vmem((2, ps * quarter, 128), BF16), vmem((2, ps, quarter, 128), BF16),
        vmem((2, quarter, 128), BF16), vmem((2, ns, piece, 128), BF16),
        dma(ns), dma(ns), dma(ns, ps), dma(ns, ps), dma(ps), dma(ps), dma(nh), dma(nh), dma(nh), dma(nh),
        dma(ns, ps), dma(ns, ps), dma(ns), dma(ns), dma(ps), dma(ps), dma(ps), dma(ps), dma(ns), dma(ns),
        dma(2, ps), dma(2, ps), dma(2, ns), dma(2, ns), dma(2, ns), dma(2, ns), dma(2, ps), dma(2, ps),
    ]
    whole = pl.BlockSpec(memory_space=pltpu.VMEM)
    scalar = pl.BlockSpec(memory_space=pltpu.SMEM)
    res, loss = pl.pallas_call(
        functools.partial(kernel, (ns, nh, ps, fs, hs, classes, piece)),
        out_shape=(
            jax.ShapeDtypeStruct((2, ps * quarter, 128), BF16),
            jax.ShapeDtypeStruct((8, 128), F32),
        ),
        in_specs=[whole, whole, scalar, scalar, whole, whole, whole, whole],
        out_specs=(whole, whole),
        scratch_shapes=scratch,
        compiler_params=pltpu.CompilerParams(
            collective_id=0, has_side_effects=True, vmem_limit_bytes=56 * 1024 * 1024
        ),
    )(tiles, labels_row, counts, offsets, wqkv, w_out, ln_gain.reshape(1, d), wcc)
    wide = res[:, :d, :].astype(F32)
    return (
        loss[0, :1], wide[0, :, :hs], wide[1, :, :hs], wide[1, :, hs:], wide[0, :, hs:].T,
    )


def solution(mesh):
    placed = (
        P(("slide", "seq", "rep"), None),
        P(("slide", "seq", "rep")),
        P(("slide", "seq", "rep")),
        P(None, "head"),
        P(None, "head"),
        P(None, "head"),
        P(None, "head"),
        P("head", None),
        P(),
        P(),
    )
    sizes = mesh.shape
    return jax.shard_map(
        functools.partial(body, sizes["seq"], sizes["head"], sizes["rep"]),
        mesh=mesh,
        in_specs=placed,
        out_specs=(
            P("slide"),
            P("slide", "head"),
            P("slide", "head"),
            P("slide", "head"),
            P("head", "slide"),
        ),
        check_vma=False,
    )
```

```python
import functools
import math

import jax
import jax.numpy as jnp
from jax import lax
from jax.experimental import pallas as pl
from jax.experimental.pallas import tpu as pltpu
from jax.sharding import PartitionSpec as P

MESH = pl.DeviceIdType.MESH
F32, BF16 = jnp.float32, jnp.bfloat16
LOW = -1e30
PERM = 256
TAIL = 16


def nn(a, b):
    return jnp.dot(a, b, preferred_element_type=F32)


def nt(a, b):
    return lax.dot_general(a, b, (((1,), (1,)), ((), ())), preferred_element_type=F32)


def tn(a, b):
    return lax.dot_general(a, b, (((0,), (0,)), ((), ())), preferred_element_type=F32)


def lanes(rows):
    return lax.broadcasted_iota(jnp.int32, (rows, 128), 1)


def subs(rows):
    return lax.broadcasted_iota(jnp.int32, (rows, 128), 0)


def three(x):
    hi = x.astype(BF16).astype(F32)
    rest = x - hi
    mid = rest.astype(BF16).astype(F32)
    return hi, mid, rest - mid


def kernel(
    dims,
    tiles, labels, counts, offsets, w_query, w_key, w_value, w_out, gain, w_class,
    res, loss_out,
    wqkv, wcc, xt, qs, kvs, ka0, va0, kv_all, ka2, va2, pr, ka1, va1, att_pk, wo,
    acc0, m0, acc1, m1, qa, doa, atb, dmix, dq, dqp, dkv, dkvp,
    rs_out, rs_sib, rs_mid, rs_z, pr_out, pr_in, lt, ltz,
    pan, pan_sib, pan_half, pan_z,
    s_far, r_far, s_fwd, r_fwd, s_pr, r_pr, s_w, r_w, s_att, r_att,
    s_rs, r_rs, s_rz, r_rz, s_pb, r_pb, s_l, r_l, s_lz, r_lz,
    s_a1, r_a1, s_a2, r_a2, s_a3, r_a3, s_a4, r_a4,
):
    ns, nh, ps, fs, hs, classes, piece = dims
    n, d = tiles.shape
    far, half = n // fs, n // ps
    sub_count = fs // ps
    z, h, p = lax.axis_index("seq"), lax.axis_index("head"), lax.axis_index("rep")

    def at_z(dz):
        return {"seq": lax.rem(z + dz, ns)}

    def at_p(dp):
        return {"rep": lax.rem(p + dp, ps)}

    def at_h(dh):
        return {"head": lax.rem(h + dh, nh)}

    sends = []

    def push(src, dst, ssem, rsem, where):
        copy = pltpu.make_async_remote_copy(
            src_ref=src, dst_ref=dst, send_sem=ssem, recv_sem=rsem,
            device_id=where, device_id_type=MESH,
        )
        copy.start()
        sends.append(copy)
        return copy

    barrier = pltpu.get_barrier_semaphore()
    peers = (
        [at_z(i) for i in range(1, ns)]
        + [at_p(i) for i in range(1, ps)]
        + [at_h(i) for i in range(1, nh)]
    )
    for peer in peers:
        pl.semaphore_signal(barrier, inc=1, device_id=peer, device_id_type=MESH)

    residues = [(c % sub_count) * ps + c // sub_count for c in range(fs)]
    count = counts[0]
    o1 = offsets[0, 0]
    o2 = offsets[0, 1]
    c2 = lax.rem(o2, ps) * sub_count + lax.div(o2, ps)

    def rows_of(c):
        return pl.ds(c * far, far)

    wqkv[pl.ds(0, hs), :] = w_query[...]
    wqkv[pl.ds(hs, hs), :] = jnp.zeros((hs, d), BF16)
    wqkv[pl.ds(2 * hs, hs), :] = w_key[...]
    wqkv[pl.ds(3 * hs, hs), :] = w_value[...]
    narrow = w_class[...].astype(F32)
    wcc[...] = jnp.concatenate([narrow, narrow], axis=0).astype(BF16)

    per = PERM // fs
    a = lax.broadcasted_iota(jnp.int32, (PERM, PERM), 0)
    b = lax.broadcasted_iota(jnp.int32, (PERM, PERM), 1)
    want = jnp.zeros((PERM, PERM), jnp.int32)
    for c in range(fs):
        want = jnp.where((a >= c * per) & (a < (c + 1) * per), (a - c * per) * fs + residues[c], want)
    perm = (want == b).astype(F32).astype(BF16)
    for blk in range(n // PERM):
        moved = nn(perm, tiles[pl.ds(blk * PERM, PERM), :]).astype(BF16)
        qkv = nt(moved, wqkv[...])
        q_part = (qkv[:, :128] * (1.0 / math.sqrt(hs))).astype(BF16)
        kv_part = qkv[:, 128:].astype(BF16)
        for c in range(fs):
            spot = pl.ds(c * far + blk * per, per)
            xt[spot, :] = moved[c * per:(c + 1) * per, :]
            qs[spot, :] = q_part[c * per:(c + 1) * per, :]
            kvs[spot, :] = kv_part[c * per:(c + 1) * per, :]

    def pick_far(ref):
        out = ref[rows_of(0), :].astype(F32)
        for c in range(1, fs):
            out = jnp.where(c2 == c, ref[rows_of(c), :].astype(F32), out)
        return out

    def pick_half(ref):
        out = ref[pl.ds(0, half), :].astype(F32)
        for c in range(1, ps):
            out = jnp.where(o1 == c, ref[pl.ds(c * half, half), :].astype(F32), out)
        return out

    high = lax.div(count, 256)
    tail = jnp.where(subs(TAIL) < 8, high.astype(F32), (count - high * 256).astype(F32)).astype(BF16)
    kv_all[0, 0, pl.ds(0, far), :] = pick_far(kvs).astype(BF16)
    kv_all[0, 0, pl.ds(far, TAIL), :] = tail
    pr[0, pl.ds(0, half), :] = pick_half(kvs).astype(BF16)
    pr[0, pl.ds(half, TAIL), :] = tail

    wo[:, pl.ds(0, hs), :] = jnp.zeros((nh, hs, d), BF16)
    wo[:, pl.ds(2 * hs, hs), :] = jnp.zeros((nh, hs, d), BF16)
    wo[0, pl.ds(hs, hs), :] = w_out[...]

    pl.semaphore_wait(barrier, len(peers))
    far_z = {}
    for dz in range(1, ns):
        far_z[dz] = push(kv_all.at[0, 0], kv_all.at[dz, 0], s_far.at[dz], r_far.at[dz], at_z(dz))
    pr_c, fwd_c, w_c, att_c = {}, {}, {}, {}
    for dp in range(1, ps):
        pr_c[dp] = push(pr.at[0], pr.at[dp], s_pr.at[dp], r_pr.at[dp], at_p(dp))
        fwd_c[0, dp] = push(kv_all.at[0, 0], kv_all.at[0, dp], s_fwd.at[0, dp], r_fwd.at[0, dp], at_p(dp))
    for dh in range(1, nh):
        w_c[dh] = push(
            wo.at[0, pl.ds(hs, hs), :], wo.at[dh, pl.ds(hs, hs), :], s_w.at[dh], r_w.at[dh], at_h(dh)
        )

    def augment(kv, original, cnt):
        rows = kv.shape[0]
        lane = lanes(rows)
        kv = kv.astype(F32)
        bias = jnp.where(original.astype(F32) < cnt, 0.0, LOW)
        key = jnp.where(lane < hs, kv, jnp.where(lane == hs, bias, 1.0))
        value = jnp.where(lane < hs, 1.0, kv)
        return key.astype(BF16), value.astype(BF16)

    def remote_count(tail):
        tail = tail.astype(F32)
        return tail[0:1, 0:1] * 256.0 + tail[8:9, 0:1]

    def with_one(q):
        return jnp.where(lanes(q.shape[0]) == hs, 1.0, q.astype(F32)).astype(BF16)

    def forward(q, key, value):
        s = nt(q, key)
        top = jnp.max(s, axis=-1, keepdims=True)
        return top, nn(jnp.exp(s - top).astype(BF16), value)

    own_count = count.astype(F32)
    step = min(256, far // 2)
    for c in range(fs):
        key, value = augment(kvs[rows_of(c), :], subs(far) * fs + residues[c], own_count)
        ka0[rows_of(c), :] = key
        va0[rows_of(c), :] = value
    wide = min(256, n)
    for i in range(n // wide):
        spot = pl.ds(i * wide, wide)
        top, acc = forward(with_one(qs[spot, :]), ka0[...], va0[...])
        m0[spot, :] = jnp.broadcast_to(top, (wide, 128))
        acc0[spot, :] = acc
    for dp in range(ps):
        if dp:
            pr_c[dp].wait_recv()
        cnt = remote_count(pr[dp, pl.ds(half, TAIL), :])
        for k in range(sub_count):
            key, value = augment(pr[dp, pl.ds(k * far, far), :], subs(far) * fs + k * ps + o1, cnt)
            ka1[pl.ds(dp * half + k * far, far), :] = key
            va1[pl.ds(dp * half + k * far, far), :] = value
    q_half = with_one(pick_half(qs))
    wide = min(256, half)
    for i in range(half // wide):
        spot = pl.ds(i * wide, wide)
        top, acc = forward(q_half[i * wide:(i + 1) * wide, :], ka1[...], va1[...])
        m1[spot, :] = jnp.broadcast_to(top, (wide, 128))
        acc1[spot, :] = acc

    q_far = with_one(pick_far(qs))
    order = [(0, dp) for dp in range(ps)]
    for dz in range(1, ns):
        order += [(dz, dp) for dp in range(ps)]
    top2 = acc2 = None
    for dz in range(1, ns):
        far_z[dz].wait_recv()
        for dp in range(1, ps):
            fwd_c[dz, dp] = push(
                kv_all.at[dz, 0], kv_all.at[dz, dp], s_fwd.at[dz, dp], r_fwd.at[dz, dp], at_p(dp)
            )
        for bz, dp in [(dz - 1, i) for i in range(ps)] + ([(dz, i) for i in range(ps)] if dz == ns - 1 else []):
            if dp:
                fwd_c[bz, dp].wait_recv()
            key, value = augment(
                kv_all[bz, dp, pl.ds(0, far), :], subs(far) * fs + o2,
                remote_count(kv_all[bz, dp, pl.ds(far, TAIL), :]),
            )
            ka2[bz * ps + dp] = key
            va2[bz * ps + dp] = value
            top, acc = forward(q_far, key, value)
            if top2 is None:
                top2, acc2 = top, acc
            else:
                both = jnp.maximum(top, top2)
                acc2 = acc2 * jnp.exp(top2 - both) + acc * jnp.exp(top - both)
                top2 = both

    for c in range(fs):
        rows = rows_of(c)
        in_half = pl.ds((c % sub_count) * far, far)
        t0 = m0[rows, 0:1]
        t1 = jnp.where(o1 == c // sub_count, m1[in_half, 0:1], LOW)
        t2 = jnp.where(c2 == c, top2, LOW)
        top = jnp.maximum(t0, jnp.maximum(t1, t2))
        acc = acc0[rows, :] * jnp.exp(t0 - top) + acc1[in_half, :] * jnp.exp(t1 - top) + acc2 * jnp.exp(t2 - top)
        total = acc[:, 0:1]
        lane = lanes(far)
        att = jnp.where(lane < hs, 0.0, acc / total)
        atb[rows, :] = att.astype(BF16)
        one, two, rest = three(-(top + jnp.log(total)))
        aux = jnp.where(lane == hs, 1.0, jnp.where(lane == hs + 1, one, jnp.where(lane == hs + 2, two, jnp.where(lane == hs + 3, rest, 0.0))))
        qa[rows, :] = jnp.where(lane < hs, qs[rows, :].astype(F32), aux).astype(BF16)
        both = pltpu.roll(att, hs, 1)[far // 2:, :] + att[:far // 2, :]
        att_pk[0, c] = both.astype(BF16)
        for dh in range(1, nh):
            att_c[c, dh] = push(att_pk.at[0, c], att_pk.at[dh, c], s_att.at[c, dh], r_att.at[c, dh], at_h(dh))
    for dh in range(1, nh):
        w_c[dh].wait_recv()

    loss = jnp.zeros((1, 1), F32)
    g = gain[...].reshape(1, d)
    span = step * fs
    marks = labels[...].reshape(1, n).astype(F32)
    pick_row = lax.broadcasted_iota(jnp.int32, (step, span), 0) * fs
    pick_col = lax.broadcasted_iota(jnp.int32, (step, span), 1)
    for i in range(n // step):
        start = i * step
        c, inner = start // far, start % far
        rows = pl.ds(start, step)
        mixed = xt[rows, :].astype(F32)
        for dh in range(nh):
            if dh and inner == 0:
                att_c[c, dh].wait_recv()
            if inner < far // 2:
                term = nn(att_pk[dh, c, pl.ds(inner, step), :], wo[dh, pl.ds(0, 2 * hs), :])
            else:
                term = nn(att_pk[dh, c, pl.ds(inner - far // 2, step), :], wo[dh, pl.ds(hs, 2 * hs), :])
            mixed = mixed + term.astype(BF16).astype(F32)
        center = mixed - jnp.mean(mixed, axis=-1, keepdims=True)
        inv_dev = lax.rsqrt(jnp.mean(center * center, axis=-1, keepdims=True) + 1e-05)
        normal = center * inv_dev
        normed = (normal * g).astype(BF16)
        logits = nt(wcc[...], normed)[:classes, :]
        peak = jnp.max(logits, axis=0, keepdims=True)
        log_total = jnp.log(jnp.sum(jnp.exp(logits - peak), axis=0, keepdims=True)) + peak
        kind = lax.broadcasted_iota(jnp.int32, (classes, step), 0).astype(F32)
        chosen = (pick_row + residues[c] == pick_col).astype(F32).astype(BF16)
        block = jnp.broadcast_to(marks[:, inner * fs:inner * fs + span], (classes, span)).astype(BF16)
        onehot = (kind == nt(block, chosen)).astype(F32)
        spot = lax.broadcasted_iota(jnp.int32, (1, step), 1)
        ok = ((spot + inner) * fs + residues[c] < count).astype(F32)
        cross = log_total - jnp.sum(onehot * logits, axis=0, keepdims=True)
        loss = loss + jnp.sum(ok * cross, axis=1, keepdims=True)
        d_logits = (jnp.exp(logits - log_total) - onehot) * ok * (1.0 / n)
        hi = d_logits.astype(BF16).astype(F32)
        split = jnp.concatenate([hi, d_logits - hi], axis=0).astype(BF16)
        d_normal = tn(split, wcc[...]) * g
        d_mixed = inv_dev * (
            d_normal
            - jnp.mean(d_normal, axis=-1, keepdims=True)
            - normal * jnp.mean(d_normal * normal, axis=-1, keepdims=True)
        )
        d_mixed = d_mixed.astype(BF16)
        dmix[rows, :] = d_mixed
        d_att = nt(d_mixed, wo[0, pl.ds(0, 2 * hs), :]).astype(BF16).astype(F32)
        delta = jnp.sum(d_att * atb[rows, :].astype(F32), axis=-1, keepdims=True)
        one, two, rest = three(-delta)
        lane = lanes(step)
        aux = jnp.where(lane == 0, one, jnp.where(lane == 1, two, jnp.where(lane == 2, rest, d_att)))
        doa[rows, :] = aux.astype(BF16)
    lt[0, :, :] = jnp.broadcast_to(loss * (1.0 / n), (8, 128))
    lt_c = {dp: push(lt.at[0], lt.at[dp], s_l.at[dp], r_l.at[dp], at_p(dp)) for dp in range(1, ps)}

    def backward(q, do, key, value):
        prob = jnp.exp(nt(key, q))
        d_score = (prob * nt(value, do)).astype(BF16)
        d_key = nn(d_score, q)
        d_value = nn(prob.astype(BF16), do)
        return tn(d_score, key), jnp.where(lanes(key.shape[0]) < hs, d_key, d_value)

    q_far = pick_far(qa).astype(BF16)
    do_far = pick_far(doa).astype(BF16)
    dq_far = None
    rz_c = {}
    own_far = None
    for dz in list(range(1, ns)) + [0]:
        rs_c = {}
        own = None
        for dp in list(range(1, ps)) + [0]:
            key_rows = dz * ps + dp
            d_q, d_kv = backward(q_far, do_far, ka2[key_rows], va2[key_rows])
            dq_far = d_q if dq_far is None else dq_far + d_q
            if dp:
                rs_out[dz, dp] = d_kv.astype(BF16)
                rs_c[dp] = push(
                    rs_out.at[dz, dp], rs_sib.at[dz, dp], s_rs.at[dz, dp], r_rs.at[dz, dp], at_p(ps - dp)
                )
            else:
                own = d_kv
        for dp in range(1, ps):
            rs_c[dp].wait_recv()
            own = own + rs_sib[dz, dp].astype(F32)
        if dz:
            rs_mid[dz] = own.astype(BF16)
            rz_c[dz] = push(rs_mid.at[dz], rs_z.at[dz], s_rz.at[dz], r_rz.at[dz], at_z(ns - dz))
        else:
            own_far = own

    whole_loss = lt[0, :, :]
    for dp in range(1, ps):
        lt_c[dp].wait_recv()
        whole_loss = whole_loss + lt[dp, :, :]
    ltz[0, :, :] = whole_loss
    lz_c = {dz: push(ltz.at[0], ltz.at[dz], s_lz.at[dz], r_lz.at[dz], at_z(dz)) for dz in range(1, ns)}

    q_half = pick_half(qa).astype(BF16)
    do_half = pick_half(doa).astype(BF16)
    pb_c = {}
    dq_half = None
    for dp in list(range(1, ps)) + [0]:
        key_rows = pl.ds(dp * half, half)
        d_q, d_kv = backward(q_half, do_half, ka1[key_rows, :], va1[key_rows, :])
        dq_half = d_q if dq_half is None else dq_half + d_q
        if dp:
            pr_out[dp] = d_kv.astype(BF16)
            pb_c[dp] = push(pr_out.at[dp], pr_in.at[dp], s_pb.at[dp], r_pb.at[dp], at_p(ps - dp))
        else:
            dkvp[...] = d_kv
    dqp[...] = dq_half

    tile = min(512, n)
    for j in range(n // tile):
        key_rows = pl.ds(j * tile, tile)
        total = None
        for i in range(n // tile):
            rows = pl.ds(i * tile, tile)
            d_q, d_kv = backward(qa[rows, :], doa[rows, :], ka0[key_rows, :], va0[key_rows, :])
            total = d_kv if total is None else total + d_kv
            if j:
                dq[rows, :] += d_q
            else:
                dq[rows, :] = d_q
        dkv[key_rows, :] = total

    for c in range(fs):
        rows = rows_of(c)
        in_half = pl.ds((c % sub_count) * far, far)
        part = dq[rows, :]
        part = part + jnp.where(o1 == c // sub_count, dqp[in_half, :], 0.0)
        part = part + jnp.where(c2 == c, dq_far, 0.0)
        qa[rows, :] = jnp.where(lanes(far) < hs, part * (1.0 / math.sqrt(hs)), 0.0).astype(BF16)

    quarter = ns * piece
    first, second, third, fourth = {}, {}, {}, {}

    def start_panel(k, panel):
        for j in range(d // 128):
            pan[k, pl.ds(j * 128, 128), :] = panel[:, j * 128:(j + 1) * 128].astype(BF16)
        if quarter * ps > d:
            pan[k, pl.ds(d, quarter * ps - d), :] = jnp.zeros((quarter * ps - d, 128), BF16)
        for dp in range(1, ps):
            there = pl.multiple_of(lax.rem(p + dp, ps) * quarter, 16)
            first[k, dp] = push(
                pan.at[k, pl.ds(there, quarter), :], pan_sib.at[k, dp],
                s_a1.at[k, dp], r_a1.at[k, dp], at_p(dp),
            )

    def second_panel(k):
        here = pl.multiple_of(p * quarter, 16)
        total = pan[k, pl.ds(here, quarter), :].astype(F32)
        for dp in range(1, ps):
            first[k, dp].wait_recv()
            total = total + pan_sib[k, dp].astype(F32)
        pan_half[k] = total.astype(BF16)
        for dz in range(1, ns):
            there = pl.multiple_of(lax.rem(z + dz, ns) * piece, 16)
            second[k, dz] = push(
                pan_half.at[k, pl.ds(there, piece), :], pan_z.at[k, dz],
                s_a2.at[k, dz], r_a2.at[k, dz], at_z(dz),
            )

    def third_panel(k):
        here = pl.multiple_of(z * piece, 16)
        total = pan_half[k, pl.ds(here, piece), :].astype(F32)
        for dz in range(1, ns):
            second[k, dz].wait_recv()
            total = total + pan_z[k, dz].astype(F32)
        spot = pl.ds(pl.multiple_of(p * quarter + z * piece, 16), piece)
        res[k, spot, :] = total.astype(BF16)
        for dz in range(1, ns):
            third[k, dz] = push(
                res.at[k, spot, :], res.at[k, spot, :], s_a3.at[k, dz], r_a3.at[k, dz], at_z(dz)
            )
        share(k, 0)

    def share(k, dz):
        spot = pl.ds(pl.multiple_of(p * quarter + lax.rem(z + ns - dz, ns) * piece, 16), piece)
        for dp in range(1, ps):
            fourth[k, dz, dp] = push(
                res.at[k, spot, :], res.at[k, spot, :], s_a4.at[k, dz, dp], r_a4.at[k, dz, dp], at_p(dp)
            )

    def fourth_panel(k):
        for dz in range(1, ns):
            third[k, dz].wait_recv()
            share(k, dz)

    start_panel(0, tn(qa[...], xt[...]) + tn(atb[...], dmix[...]))

    half_sum = dkvp[...]
    for dp in range(1, ps):
        pb_c[dp].wait_recv()
        half_sum = half_sum + pr_in[dp].astype(F32)
    dkvp[...] = half_sum
    second_panel(0)
    for dz in range(1, ns):
        rz_c[dz].wait_recv()
        own_far = own_far + rs_z[dz].astype(F32)
    for c in range(fs):
        rows = rows_of(c)
        in_half = pl.ds((c % sub_count) * far, far)
        part = dkv[rows, :]
        part = part + jnp.where(o1 == c // sub_count, dkvp[in_half, :], 0.0)
        part = part + jnp.where(c2 == c, own_far, 0.0)
        doa[rows, :] = part.astype(BF16)
    start_panel(1, tn(doa[...], xt[...]))
    third_panel(0)
    second_panel(1)
    fourth_panel(0)
    third_panel(1)
    total = ltz[0, :, :]
    for dz in range(1, ns):
        lz_c[dz].wait_recv()
        total = total + ltz[dz, :, :]
    loss_out[...] = total
    fourth_panel(1)
    for k in range(2):
        for dz in range(ns):
            for dp in range(1, ps):
                fourth[k, dz, dp].wait_recv()
    for copy in sends:
        copy.wait_send()


def unpack(hs, res, loss, tile_loss, g_query, g_key, g_value, g_out):
    tile_loss[0] = loss[0, 0]
    for j in range(g_query.shape[1] // 128):
        cols = pl.ds(j * 128, 128)
        g_query[:, cols] = res[0, pl.ds(j * 128, hs), :].astype(F32)
        g_out[:, cols] = res[0, pl.ds(j * 128 + hs, hs), :].astype(F32)
        g_key[:, cols] = res[1, pl.ds(j * 128, hs), :].astype(F32)
        g_value[:, cols] = res[1, pl.ds(j * 128 + hs, hs), :].astype(F32)


def body(ns, nh, ps, tiles, labels, counts, offsets, w_query, w_key, w_value, w_out, ln_gain, w_class):
    n, d = tiles.shape
    hs = w_query.shape[1]
    classes = w_class.shape[1]
    shards = ns * ps
    fs = shards // 4
    far, half = n // fs, n // ps
    piece = -(-d // (shards * 16)) * 16
    quarter = ns * piece
    vmem = pltpu.VMEM
    dma = lambda *shape: pltpu.SemaphoreType.DMA(shape)
    scratch = [
        vmem((4 * hs, d), BF16), vmem((2 * classes, d), BF16),
        vmem((n, d), BF16), vmem((n, 128), BF16), vmem((n, 128), BF16),
        vmem((n, 128), BF16), vmem((n, 128), BF16),
        vmem((ns, ps, far + TAIL, 128), BF16),
        vmem((shards, far, 128), BF16), vmem((shards, far, 128), BF16),
        vmem((ps, half + TAIL, 128), BF16), vmem((n, 128), BF16), vmem((n, 128), BF16),
        vmem((nh, fs, far // 2, 128), BF16), vmem((nh, 3 * hs, d), BF16),
        vmem((n, 128), F32), vmem((n, 128), F32), vmem((half, 128), F32), vmem((half, 128), F32),
        vmem((n, 128), BF16), vmem((n, 128), BF16), vmem((n, 128), BF16), vmem((n, d), BF16),
        vmem((n, 128), F32), vmem((half, 128), F32), vmem((n, 128), F32), vmem((half, 128), F32),
        vmem((ns, ps, far, 128), BF16), vmem((ns, ps, far, 128), BF16),
        vmem((ns, far, 128), BF16), vmem((ns, far, 128), BF16),
        vmem((ps, half, 128), BF16), vmem((ps, half, 128), BF16),
        vmem((ps, 8, 128), F32), vmem((ns, 8, 128), F32),
        vmem((2, ps * quarter, 128), BF16), vmem((2, ps, quarter, 128), BF16),
        vmem((2, quarter, 128), BF16), vmem((2, ns, piece, 128), BF16),
        dma(ns), dma(ns), dma(ns, ps), dma(ns, ps), dma(ps), dma(ps), dma(nh), dma(nh), dma(fs, nh), dma(fs, nh),
        dma(ns, ps), dma(ns, ps), dma(ns), dma(ns), dma(ps), dma(ps), dma(ps), dma(ps), dma(ns), dma(ns),
        dma(2, ps), dma(2, ps), dma(2, ns), dma(2, ns), dma(2, ns), dma(2, ns), dma(2, ns, ps), dma(2, ns, ps),
    ]
    whole = pl.BlockSpec(memory_space=pltpu.VMEM)
    scalar = pl.BlockSpec(memory_space=pltpu.SMEM)
    res, loss = pl.pallas_call(
        functools.partial(kernel, (ns, nh, ps, fs, hs, classes, piece)),
        out_shape=(
            jax.ShapeDtypeStruct((2, ps * quarter, 128), BF16),
            jax.ShapeDtypeStruct((8, 128), F32),
        ),
        in_specs=[whole, whole, scalar, scalar] + [whole] * 6,
        out_specs=(whole, whole),
        scratch_shapes=scratch,
        compiler_params=pltpu.CompilerParams(
            collective_id=0, has_side_effects=True, vmem_limit_bytes=56 * 1024 * 1024
        ),
    )(tiles, labels, counts, offsets.T, w_query.T, w_key.T, w_value.T, w_out, ln_gain, w_class.T)
    flat = jax.ShapeDtypeStruct((hs, d), F32)
    tile_loss, g_query, g_key, g_value, g_out = pl.pallas_call(
        functools.partial(unpack, hs),
        out_shape=(jax.ShapeDtypeStruct((1,), F32), flat, flat, flat, flat),
        in_specs=[whole, whole],
        out_specs=(scalar, whole, whole, whole, whole),
    )(res, loss)
    return (tile_loss, g_query.T, g_key.T, g_value.T, g_out)


def solution(mesh):
    placed = (
        P(("slide", "seq", "rep"), None),
        P(("slide", "seq", "rep")),
        P(("slide", "seq", "rep")),
        P(None, "head"),
        P(None, "head"),
        P(None, "head"),
        P(None, "head"),
        P("head", None),
        P(),
        P(),
    )
    sizes = mesh.shape
    return jax.shard_map(
        functools.partial(body, sizes["seq"], sizes["head"], sizes["rep"]),
        mesh=mesh,
        in_specs=placed,
        out_specs=(
            P("slide"),
            P("slide", "head"),
            P("slide", "head"),
            P("slide", "head"),
            P("head", "slide"),
        ),
        check_vma=False,
    )
```

```python
import functools
import math

import jax
import jax.numpy as jnp
from jax import lax
from jax.experimental import pallas as pl
from jax.experimental.pallas import tpu as pltpu
from jax.sharding import PartitionSpec as P

MESH = pl.DeviceIdType.MESH
F32, BF16 = jnp.float32, jnp.bfloat16
LOW = -1e30
PERM = 256
TAIL = 16


def nn(a, b):
    return jnp.dot(a, b, preferred_element_type=F32)


def nt(a, b):
    return lax.dot_general(a, b, (((1,), (1,)), ((), ())), preferred_element_type=F32)


def tn(a, b):
    return lax.dot_general(a, b, (((0,), (0,)), ((), ())), preferred_element_type=F32)


def lanes(rows):
    return lax.broadcasted_iota(jnp.int32, (rows, 128), 1)


def subs(rows):
    return lax.broadcasted_iota(jnp.int32, (rows, 128), 0)


def three(x):
    hi = x.astype(BF16).astype(F32)
    rest = x - hi
    mid = rest.astype(BF16).astype(F32)
    return hi, mid, rest - mid


def kernel(
    dims,
    tiles, labels, counts, offsets, w_query, w_key, w_value, w_out, gain, w_class,
    res, loss_out,
    wqkv, wcc, xt, qs, kvs, ka0, va0, kv_all, ka2, va2, pr, ka1, va1, att_pk, wo,
    acc0, m0, acc1, m1, qa, doa, atb, dmix, dq, dqp, dkv, dkvp,
    rs_out, rs_sib, rs_mid, rs_z, pr_out, pr_in, lt, ltz,
    pan, pan_sib, pan_half, pan_z,
    s_far, r_far, s_fwd, r_fwd, s_pr, r_pr, s_w, r_w, s_att, r_att,
    s_rs, r_rs, s_rz, r_rz, s_pb, r_pb, s_l, r_l, s_lz, r_lz,
    s_a1, r_a1, s_a2, r_a2, s_a3, r_a3, s_a4, r_a4,
):
    ns, nh, ps, fs, hs, classes, piece = dims
    n, d = tiles.shape
    far, half = n // fs, n // ps
    sub_count = fs // ps
    z, h, p = lax.axis_index("seq"), lax.axis_index("head"), lax.axis_index("rep")

    def at_z(dz):
        return {"seq": lax.rem(z + dz, ns)}

    def at_x(e):
        place, bit = z, 1
        while bit < ns:
            if e & bit:
                place = place + bit - 2 * bit * lax.rem(lax.div(z, bit), 2)
            bit *= 2
        return {"seq": place}

    def at_p(dp):
        return {"rep": lax.rem(p + dp, ps)}

    def at_h(dh):
        return {"head": lax.rem(h + dh, nh)}

    sends = []

    def push(src, dst, ssem, rsem, where):
        copy = pltpu.make_async_remote_copy(
            src_ref=src, dst_ref=dst, send_sem=ssem, recv_sem=rsem,
            device_id=where, device_id_type=MESH,
        )
        copy.start()
        sends.append(copy)
        return copy

    barrier = pltpu.get_barrier_semaphore()
    peers = (
        [at_z(i) for i in range(1, ns)]
        + [at_p(i) for i in range(1, ps)]
        + [at_h(i) for i in range(1, nh)]
    )
    for peer in peers:
        pl.semaphore_signal(barrier, inc=1, device_id=peer, device_id_type=MESH)

    residues = [(c % sub_count) * ps + c // sub_count for c in range(fs)]
    count = counts[0]
    o1 = offsets[0, 0]
    o2 = offsets[0, 1]
    c2 = lax.rem(o2, ps) * sub_count + lax.div(o2, ps)

    def rows_of(c):
        return pl.ds(c * far, far)

    wqkv[pl.ds(0, hs), :] = w_query[...]
    wqkv[pl.ds(hs, hs), :] = jnp.zeros((hs, d), BF16)
    wqkv[pl.ds(2 * hs, hs), :] = w_key[...]
    wqkv[pl.ds(3 * hs, hs), :] = w_value[...]
    narrow = w_class[...].astype(F32)
    wcc[...] = jnp.concatenate([narrow, narrow], axis=0).astype(BF16)

    per = PERM // fs
    a = lax.broadcasted_iota(jnp.int32, (PERM, PERM), 0)
    b = lax.broadcasted_iota(jnp.int32, (PERM, PERM), 1)
    want = jnp.zeros((PERM, PERM), jnp.int32)
    for c in range(fs):
        want = jnp.where((a >= c * per) & (a < (c + 1) * per), (a - c * per) * fs + residues[c], want)
    perm = (want == b).astype(F32).astype(BF16)
    for blk in range(n // PERM):
        moved = nn(perm, tiles[pl.ds(blk * PERM, PERM), :]).astype(BF16)
        qkv = nt(moved, wqkv[...])
        q_part = (qkv[:, :128] * (1.0 / math.sqrt(hs))).astype(BF16)
        kv_part = qkv[:, 128:].astype(BF16)
        for c in range(fs):
            spot = pl.ds(c * far + blk * per, per)
            xt[spot, :] = moved[c * per:(c + 1) * per, :]
            qs[spot, :] = q_part[c * per:(c + 1) * per, :]
            kvs[spot, :] = kv_part[c * per:(c + 1) * per, :]

    def pick_far(ref):
        out = ref[rows_of(0), :].astype(F32)
        for c in range(1, fs):
            out = jnp.where(c2 == c, ref[rows_of(c), :].astype(F32), out)
        return out

    def pick_half(ref):
        out = ref[pl.ds(0, half), :].astype(F32)
        for c in range(1, ps):
            out = jnp.where(o1 == c, ref[pl.ds(c * half, half), :].astype(F32), out)
        return out

    high = lax.div(count, 256)
    tail = jnp.where(subs(TAIL) < 8, high.astype(F32), (count - high * 256).astype(F32)).astype(BF16)
    kv_all[0, 0, pl.ds(0, far), :] = pick_far(kvs).astype(BF16)
    kv_all[0, 0, pl.ds(far, TAIL), :] = tail
    pr[0, pl.ds(0, half), :] = pick_half(kvs).astype(BF16)
    pr[0, pl.ds(half, TAIL), :] = tail

    wo[:, pl.ds(0, hs), :] = jnp.zeros((nh, hs, d), BF16)
    wo[:, pl.ds(2 * hs, hs), :] = jnp.zeros((nh, hs, d), BF16)
    wo[0, pl.ds(hs, hs), :] = w_out[...]

    pl.semaphore_wait(barrier, len(peers))
    far_z = {}
    for e in list(range(2, ns, 2)) + [1]:
        far_z[e] = push(kv_all.at[0, 0], kv_all.at[e, 0], s_far.at[e], r_far.at[e], at_x(e))
    pr_c, fwd_c, w_c, att_c = {}, {}, {}, {}
    for dp in range(1, ps):
        pr_c[dp] = push(pr.at[0], pr.at[dp], s_pr.at[dp], r_pr.at[dp], at_p(dp))
        fwd_c[0, dp] = push(kv_all.at[0, 0], kv_all.at[0, dp], s_fwd.at[0, dp], r_fwd.at[0, dp], at_p(dp))
    for dh in range(1, nh):
        w_c[dh] = push(
            wo.at[0, pl.ds(hs, hs), :], wo.at[dh, pl.ds(hs, hs), :], s_w.at[dh], r_w.at[dh], at_h(dh)
        )

    def augment(kv, original, cnt):
        rows = kv.shape[0]
        lane = lanes(rows)
        kv = kv.astype(F32)
        bias = jnp.where(original.astype(F32) < cnt, 0.0, LOW)
        key = jnp.where(lane < hs, kv, jnp.where(lane == hs, bias, 1.0))
        value = jnp.where(lane < hs, 1.0, kv)
        return key.astype(BF16), value.astype(BF16)

    def remote_count(tail):
        tail = tail.astype(F32)
        return tail[0:1, 0:1] * 256.0 + tail[8:9, 0:1]

    def with_one(q):
        return jnp.where(lanes(q.shape[0]) == hs, 1.0, q.astype(F32)).astype(BF16)

    def forward(q, key, value):
        s = nt(q, key)
        top = jnp.max(s, axis=-1, keepdims=True)
        return top, nn(jnp.exp(s - top).astype(BF16), value)

    own_count = count.astype(F32)
    step = min(256, far // 2)
    for c in range(fs):
        key, value = augment(kvs[rows_of(c), :], subs(far) * fs + residues[c], own_count)
        ka0[rows_of(c), :] = key
        va0[rows_of(c), :] = value
    wide = min(256, n)
    for i in range(n // wide):
        spot = pl.ds(i * wide, wide)
        top, acc = forward(with_one(qs[spot, :]), ka0[...], va0[...])
        m0[spot, :] = jnp.broadcast_to(top, (wide, 128))
        acc0[spot, :] = acc
    for dp in range(ps):
        if dp:
            pr_c[dp].wait_recv()
        cnt = remote_count(pr[dp, pl.ds(half, TAIL), :])
        for k in range(sub_count):
            key, value = augment(pr[dp, pl.ds(k * far, far), :], subs(far) * fs + k * ps + o1, cnt)
            ka1[pl.ds(dp * half + k * far, far), :] = key
            va1[pl.ds(dp * half + k * far, far), :] = value
    q_half = with_one(pick_half(qs))
    wide = min(256, half)
    for i in range(half // wide):
        spot = pl.ds(i * wide, wide)
        top, acc = forward(q_half[i * wide:(i + 1) * wide, :], ka1[...], va1[...])
        m1[spot, :] = jnp.broadcast_to(top, (wide, 128))
        acc1[spot, :] = acc

    q_far = with_one(pick_far(qs))
    running = [None, None]

    def arrived(e):
        far_z[e].wait_recv()
        if e and e % 2 == 0:
            far_z[e + 1] = push(
                kv_all.at[e, 0], kv_all.at[e + 1, 0], s_far.at[e + 1], r_far.at[e + 1], at_x(1)
            )
        for dp in range(1, ps):
            fwd_c[e, dp] = push(
                kv_all.at[e, 0], kv_all.at[e, dp], s_fwd.at[e, dp], r_fwd.at[e, dp], at_p(dp)
            )

    def use(e):
        for dp in range(ps):
            if dp:
                fwd_c[e, dp].wait_recv()
            key, value = augment(
                kv_all[e, dp, pl.ds(0, far), :], subs(far) * fs + o2,
                remote_count(kv_all[e, dp, pl.ds(far, TAIL), :]),
            )
            ka2[e * ps + dp] = key
            va2[e * ps + dp] = value
            top, acc = forward(q_far, key, value)
            if running[0] is not None:
                both = jnp.maximum(top, running[0])
                acc = running[1] * jnp.exp(running[0] - both) + acc * jnp.exp(top - both)
                top = both
            running[:] = [top, acc]

    arrived(1)
    use(0)
    for e in range(2, ns, 2):
        arrived(e)
        use(e - 1)
        use(e)
        arrived(e + 1)
    use(ns - 1)
    top2, acc2 = running

    for c in range(fs):
        rows = rows_of(c)
        in_half = pl.ds((c % sub_count) * far, far)
        t0 = m0[rows, 0:1]
        t1 = jnp.where(o1 == c // sub_count, m1[in_half, 0:1], LOW)
        t2 = jnp.where(c2 == c, top2, LOW)
        top = jnp.maximum(t0, jnp.maximum(t1, t2))
        acc = acc0[rows, :] * jnp.exp(t0 - top) + acc1[in_half, :] * jnp.exp(t1 - top) + acc2 * jnp.exp(t2 - top)
        total = acc[:, 0:1]
        lane = lanes(far)
        att = jnp.where(lane < hs, 0.0, acc / total)
        atb[rows, :] = att.astype(BF16)
        one, two, rest = three(-(top + jnp.log(total)))
        aux = jnp.where(lane == hs, 1.0, jnp.where(lane == hs + 1, one, jnp.where(lane == hs + 2, two, jnp.where(lane == hs + 3, rest, 0.0))))
        qa[rows, :] = jnp.where(lane < hs, qs[rows, :].astype(F32), aux).astype(BF16)
        both = pltpu.roll(att, hs, 1)[far // 2:, :] + att[:far // 2, :]
        att_pk[0, c] = both.astype(BF16)
        for dh in range(1, nh):
            att_c[c, dh] = push(att_pk.at[0, c], att_pk.at[dh, c], s_att.at[c, dh], r_att.at[c, dh], at_h(dh))
    for dh in range(1, nh):
        w_c[dh].wait_recv()

    loss = jnp.zeros((1, 1), F32)
    g = gain[...].reshape(1, d)
    span = step * fs
    marks = labels[...].reshape(1, n).astype(F32)
    pick_row = lax.broadcasted_iota(jnp.int32, (step, span), 0) * fs
    pick_col = lax.broadcasted_iota(jnp.int32, (step, span), 1)
    for i in range(n // step):
        start = i * step
        c, inner = start // far, start % far
        rows = pl.ds(start, step)
        mixed = xt[rows, :].astype(F32)
        for dh in range(nh):
            if dh and inner == 0:
                att_c[c, dh].wait_recv()
            if inner < far // 2:
                term = nn(att_pk[dh, c, pl.ds(inner, step), :], wo[dh, pl.ds(0, 2 * hs), :])
            else:
                term = nn(att_pk[dh, c, pl.ds(inner - far // 2, step), :], wo[dh, pl.ds(hs, 2 * hs), :])
            mixed = mixed + term.astype(BF16).astype(F32)
        center = mixed - jnp.mean(mixed, axis=-1, keepdims=True)
        inv_dev = lax.rsqrt(jnp.mean(center * center, axis=-1, keepdims=True) + 1e-05)
        normal = center * inv_dev
        normed = (normal * g).astype(BF16)
        logits = nt(wcc[...], normed)[:classes, :]
        peak = jnp.max(logits, axis=0, keepdims=True)
        log_total = jnp.log(jnp.sum(jnp.exp(logits - peak), axis=0, keepdims=True)) + peak
        kind = lax.broadcasted_iota(jnp.int32, (classes, step), 0).astype(F32)
        chosen = (pick_row + residues[c] == pick_col).astype(F32).astype(BF16)
        block = jnp.broadcast_to(marks[:, inner * fs:inner * fs + span], (classes, span)).astype(BF16)
        onehot = (kind == nt(block, chosen)).astype(F32)
        spot = lax.broadcasted_iota(jnp.int32, (1, step), 1)
        ok = ((spot + inner) * fs + residues[c] < count).astype(F32)
        cross = log_total - jnp.sum(onehot * logits, axis=0, keepdims=True)
        loss = loss + jnp.sum(ok * cross, axis=1, keepdims=True)
        d_logits = (jnp.exp(logits - log_total) - onehot) * ok * (1.0 / n)
        hi = d_logits.astype(BF16).astype(F32)
        split = jnp.concatenate([hi, d_logits - hi], axis=0).astype(BF16)
        d_normal = tn(split, wcc[...]) * g
        d_mixed = inv_dev * (
            d_normal
            - jnp.mean(d_normal, axis=-1, keepdims=True)
            - normal * jnp.mean(d_normal * normal, axis=-1, keepdims=True)
        )
        d_mixed = d_mixed.astype(BF16)
        dmix[rows, :] = d_mixed
        d_att = nt(d_mixed, wo[0, pl.ds(0, 2 * hs), :]).astype(BF16).astype(F32)
        delta = jnp.sum(d_att * atb[rows, :].astype(F32), axis=-1, keepdims=True)
        one, two, rest = three(-delta)
        lane = lanes(step)
        aux = jnp.where(lane == 0, one, jnp.where(lane == 1, two, jnp.where(lane == 2, rest, d_att)))
        doa[rows, :] = aux.astype(BF16)
    lt[0, :, :] = jnp.broadcast_to(loss * (1.0 / n), (8, 128))
    lt_c = {dp: push(lt.at[0], lt.at[dp], s_l.at[dp], r_l.at[dp], at_p(dp)) for dp in range(1, ps)}

    def backward(q, do, key, value):
        prob = jnp.exp(nt(key, q))
        d_score = (prob * nt(value, do)).astype(BF16)
        d_key = nn(d_score, q)
        d_value = nn(prob.astype(BF16), do)
        return tn(d_score, key), jnp.where(lanes(key.shape[0]) < hs, d_key, d_value)

    q_far = pick_far(qa).astype(BF16)
    do_far = pick_far(doa).astype(BF16)
    dq_far = None
    rz_c, rs_c, own = {}, {}, {}

    def settle(e):
        total = own[e]
        for dp in range(1, ps):
            rs_c[e, dp].wait_recv()
            total = total + rs_sib[e, dp].astype(F32)
        own[e] = total
        if e % 2:
            rs_mid[e] = total.astype(BF16)
            rz_c[e] = push(rs_mid.at[e], rs_z.at[e], s_rz.at[e], r_rz.at[e], at_x(1))

    turns = list(range(3, ns, 2)) + list(range(2, ns, 2)) + [1, 0]
    for turn, e in enumerate(turns):
        for dp in list(range(1, ps)) + [0]:
            if dp == 0 and turn:
                settle(turns[turn - 1])
            key_rows = e * ps + dp
            d_q, d_kv = backward(q_far, do_far, ka2[key_rows], va2[key_rows])
            dq_far = d_q if dq_far is None else dq_far + d_q
            if dp:
                rs_out[e, dp] = d_kv.astype(BF16)
                rs_c[e, dp] = push(
                    rs_out.at[e, dp], rs_sib.at[e, dp], s_rs.at[e, dp], r_rs.at[e, dp], at_p(ps - dp)
                )
            else:
                own[e] = d_kv
    for e in range(2, ns, 2):
        rz_c[e + 1].wait_recv()
        rs_mid[e] = (own[e] + rs_z[e + 1].astype(F32)).astype(BF16)
        rz_c[e] = push(rs_mid.at[e], rs_z.at[e], s_rz.at[e], r_rz.at[e], at_x(e))

    whole_loss = lt[0, :, :]
    for dp in range(1, ps):
        lt_c[dp].wait_recv()
        whole_loss = whole_loss + lt[dp, :, :]
    ltz[0, :, :] = whole_loss
    lz_c = {dz: push(ltz.at[0], ltz.at[dz], s_lz.at[dz], r_lz.at[dz], at_z(dz)) for dz in range(1, ns)}

    q_half = pick_half(qa).astype(BF16)
    do_half = pick_half(doa).astype(BF16)
    pb_c = {}
    dq_half = None
    for dp in list(range(1, ps)) + [0]:
        key_rows = pl.ds(dp * half, half)
        d_q, d_kv = backward(q_half, do_half, ka1[key_rows, :], va1[key_rows, :])
        dq_half = d_q if dq_half is None else dq_half + d_q
        if dp:
            pr_out[dp] = d_kv.astype(BF16)
            pb_c[dp] = push(pr_out.at[dp], pr_in.at[dp], s_pb.at[dp], r_pb.at[dp], at_p(ps - dp))
        else:
            dkvp[...] = d_kv
    dqp[...] = dq_half

    tile = min(512, n)
    for j in range(n // tile):
        key_rows = pl.ds(j * tile, tile)
        total = None
        for i in range(n // tile):
            rows = pl.ds(i * tile, tile)
            d_q, d_kv = backward(qa[rows, :], doa[rows, :], ka0[key_rows, :], va0[key_rows, :])
            total = d_kv if total is None else total + d_kv
            if j:
                dq[rows, :] += d_q
            else:
                dq[rows, :] = d_q
        dkv[key_rows, :] = total

    for c in range(fs):
        rows = rows_of(c)
        in_half = pl.ds((c % sub_count) * far, far)
        part = dq[rows, :]
        part = part + jnp.where(o1 == c // sub_count, dqp[in_half, :], 0.0)
        part = part + jnp.where(c2 == c, dq_far, 0.0)
        qa[rows, :] = jnp.where(lanes(far) < hs, part * (1.0 / math.sqrt(hs)), 0.0).astype(BF16)

    quarter = ns * piece
    first, second, third, fourth = {}, {}, {}, {}

    def start_panel(k, panel):
        for j in range(d // 128):
            pan[k, pl.ds(j * 128, 128), :] = panel[:, j * 128:(j + 1) * 128].astype(BF16)
        if quarter * ps > d:
            pan[k, pl.ds(d, quarter * ps - d), :] = jnp.zeros((quarter * ps - d, 128), BF16)
        for dp in range(1, ps):
            there = pl.multiple_of(lax.rem(p + dp, ps) * quarter, 16)
            first[k, dp] = push(
                pan.at[k, pl.ds(there, quarter), :], pan_sib.at[k, dp],
                s_a1.at[k, dp], r_a1.at[k, dp], at_p(dp),
            )

    def second_panel(k):
        here = pl.multiple_of(p * quarter, 16)
        total = pan[k, pl.ds(here, quarter), :].astype(F32)
        for dp in range(1, ps):
            first[k, dp].wait_recv()
            total = total + pan_sib[k, dp].astype(F32)
        pan_half[k] = total.astype(BF16)
        for dz in range(1, ns):
            there = pl.multiple_of(lax.rem(z + dz, ns) * piece, 16)
            second[k, dz] = push(
                pan_half.at[k, pl.ds(there, piece), :], pan_z.at[k, dz],
                s_a2.at[k, dz], r_a2.at[k, dz], at_z(dz),
            )

    def third_panel(k):
        here = pl.multiple_of(z * piece, 16)
        total = pan_half[k, pl.ds(here, piece), :].astype(F32)
        for dz in range(1, ns):
            second[k, dz].wait_recv()
            total = total + pan_z[k, dz].astype(F32)
        spot = pl.ds(pl.multiple_of(p * quarter + z * piece, 16), piece)
        res[k, spot, :] = total.astype(BF16)
        for dz in range(1, ns):
            third[k, dz] = push(
                res.at[k, spot, :], res.at[k, spot, :], s_a3.at[k, dz], r_a3.at[k, dz], at_z(dz)
            )
        share(k, 0)

    def share(k, dz):
        spot = pl.ds(pl.multiple_of(p * quarter + lax.rem(z + ns - dz, ns) * piece, 16), piece)
        for dp in range(1, ps):
            fourth[k, dz, dp] = push(
                res.at[k, spot, :], res.at[k, spot, :], s_a4.at[k, dz, dp], r_a4.at[k, dz, dp], at_p(dp)
            )

    def fourth_panel(k):
        for dz in range(1, ns):
            third[k, dz].wait_recv()
            share(k, dz)

    start_panel(0, tn(qa[...], xt[...]) + tn(atb[...], dmix[...]))

    half_sum = dkvp[...]
    for dp in range(1, ps):
        pb_c[dp].wait_recv()
        half_sum = half_sum + pr_in[dp].astype(F32)
    dkvp[...] = half_sum
    second_panel(0)
    settle(0)
    own_far = own[0]
    for e in [1] + list(range(2, ns, 2)):
        rz_c[e].wait_recv()
        own_far = own_far + rs_z[e].astype(F32)
    for c in range(fs):
        rows = rows_of(c)
        in_half = pl.ds((c % sub_count) * far, far)
        part = dkv[rows, :]
        part = part + jnp.where(o1 == c // sub_count, dkvp[in_half, :], 0.0)
        part = part + jnp.where(c2 == c, own_far, 0.0)
        doa[rows, :] = part.astype(BF16)
    start_panel(1, tn(doa[...], xt[...]))
    third_panel(0)
    second_panel(1)
    fourth_panel(0)
    third_panel(1)
    total = ltz[0, :, :]
    for dz in range(1, ns):
        lz_c[dz].wait_recv()
        total = total + ltz[dz, :, :]
    loss_out[...] = total
    fourth_panel(1)
    for k in range(2):
        for dz in range(ns):
            for dp in range(1, ps):
                fourth[k, dz, dp].wait_recv()
    for copy in sends:
        copy.wait_send()


def unpack(hs, res, loss, tile_loss, g_query, g_key, g_value, g_out):
    tile_loss[0] = loss[0, 0]
    for j in range(g_query.shape[1] // 128):
        cols = pl.ds(j * 128, 128)
        g_query[:, cols] = res[0, pl.ds(j * 128, hs), :].astype(F32)
        g_out[:, cols] = res[0, pl.ds(j * 128 + hs, hs), :].astype(F32)
        g_key[:, cols] = res[1, pl.ds(j * 128, hs), :].astype(F32)
        g_value[:, cols] = res[1, pl.ds(j * 128 + hs, hs), :].astype(F32)


def body(ns, nh, ps, tiles, labels, counts, offsets, w_query, w_key, w_value, w_out, ln_gain, w_class):
    n, d = tiles.shape
    hs = w_query.shape[1]
    classes = w_class.shape[1]
    shards = ns * ps
    fs = shards // 4
    far, half = n // fs, n // ps
    piece = -(-d // (shards * 16)) * 16
    quarter = ns * piece
    vmem = pltpu.VMEM
    dma = lambda *shape: pltpu.SemaphoreType.DMA(shape)
    scratch = [
        vmem((4 * hs, d), BF16), vmem((2 * classes, d), BF16),
        vmem((n, d), BF16), vmem((n, 128), BF16), vmem((n, 128), BF16),
        vmem((n, 128), BF16), vmem((n, 128), BF16),
        vmem((ns, ps, far + TAIL, 128), BF16),
        vmem((shards, far, 128), BF16), vmem((shards, far, 128), BF16),
        vmem((ps, half + TAIL, 128), BF16), vmem((n, 128), BF16), vmem((n, 128), BF16),
        vmem((nh, fs, far // 2, 128), BF16), vmem((nh, 3 * hs, d), BF16),
        vmem((n, 128), F32), vmem((n, 128), F32), vmem((half, 128), F32), vmem((half, 128), F32),
        vmem((n, 128), BF16), vmem((n, 128), BF16), vmem((n, 128), BF16), vmem((n, d), BF16),
        vmem((n, 128), F32), vmem((half, 128), F32), vmem((n, 128), F32), vmem((half, 128), F32),
        vmem((ns, ps, far, 128), BF16), vmem((ns, ps, far, 128), BF16),
        vmem((ns, far, 128), BF16), vmem((ns, far, 128), BF16),
        vmem((ps, half, 128), BF16), vmem((ps, half, 128), BF16),
        vmem((ps, 8, 128), F32), vmem((ns, 8, 128), F32),
        vmem((2, ps * quarter, 128), BF16), vmem((2, ps, quarter, 128), BF16),
        vmem((2, quarter, 128), BF16), vmem((2, ns, piece, 128), BF16),
        dma(ns), dma(ns), dma(ns, ps), dma(ns, ps), dma(ps), dma(ps), dma(nh), dma(nh), dma(fs, nh), dma(fs, nh),
        dma(ns, ps), dma(ns, ps), dma(ns), dma(ns), dma(ps), dma(ps), dma(ps), dma(ps), dma(ns), dma(ns),
        dma(2, ps), dma(2, ps), dma(2, ns), dma(2, ns), dma(2, ns), dma(2, ns), dma(2, ns, ps), dma(2, ns, ps),
    ]
    whole = pl.BlockSpec(memory_space=pltpu.VMEM)
    scalar = pl.BlockSpec(memory_space=pltpu.SMEM)
    res, loss = pl.pallas_call(
        functools.partial(kernel, (ns, nh, ps, fs, hs, classes, piece)),
        out_shape=(
            jax.ShapeDtypeStruct((2, ps * quarter, 128), BF16),
            jax.ShapeDtypeStruct((8, 128), F32),
        ),
        in_specs=[whole, whole, scalar, scalar] + [whole] * 6,
        out_specs=(whole, whole),
        scratch_shapes=scratch,
        compiler_params=pltpu.CompilerParams(
            collective_id=0, has_side_effects=True, vmem_limit_bytes=56 * 1024 * 1024
        ),
    )(tiles, labels, counts, offsets.T, w_query.T, w_key.T, w_value.T, w_out, ln_gain, w_class.T)
    flat = jax.ShapeDtypeStruct((hs, d), F32)
    tile_loss, g_query, g_key, g_value, g_out = pl.pallas_call(
        functools.partial(unpack, hs),
        out_shape=(jax.ShapeDtypeStruct((1,), F32), flat, flat, flat, flat),
        in_specs=[whole, whole],
        out_specs=(scalar, whole, whole, whole, whole),
    )(res, loss)
    return (tile_loss, g_query.T, g_key.T, g_value.T, g_out)


def solution(mesh):
    placed = (
        P(("slide", "seq", "rep"), None),
        P(("slide", "seq", "rep")),
        P(("slide", "seq", "rep")),
        P(None, "head"),
        P(None, "head"),
        P(None, "head"),
        P(None, "head"),
        P("head", None),
        P(),
        P(),
    )
    sizes = mesh.shape
    return jax.shard_map(
        functools.partial(body, sizes["seq"], sizes["head"], sizes["rep"]),
        mesh=mesh,
        in_specs=placed,
        out_specs=(
            P("slide"),
            P("slide", "head"),
            P("slide", "head"),
            P("slide", "head"),
            P("head", "slide"),
        ),
        check_vma=False,
    )
```

```python
import functools
import math

import jax
import jax.numpy as jnp
from jax import lax
from jax.experimental import pallas as pl
from jax.experimental.pallas import tpu as pltpu
from jax.sharding import PartitionSpec as P

MESH = pl.DeviceIdType.MESH
F32, BF16 = jnp.float32, jnp.bfloat16
LOW = -1e30
PERM = 256
TAIL = 16


def nn(a, b):
    return jnp.dot(a, b, preferred_element_type=F32)


def nt(a, b):
    return lax.dot_general(a, b, (((1,), (1,)), ((), ())), preferred_element_type=F32)


def tn(a, b):
    return lax.dot_general(a, b, (((0,), (0,)), ((), ())), preferred_element_type=F32)


def lanes(rows):
    return lax.broadcasted_iota(jnp.int32, (rows, 128), 1)


def subs(rows):
    return lax.broadcasted_iota(jnp.int32, (rows, 128), 0)


def three(x):
    hi = x.astype(BF16).astype(F32)
    rest = x - hi
    mid = rest.astype(BF16).astype(F32)
    return hi, mid, rest - mid


def kernel(
    dims,
    tiles, labels, counts, offsets, w_query, w_key, w_value, w_out, gain, w_class,
    res, loss_out,
    wqkv, wcc, xt, qs, kvs, ka0, va0, kv_all, ka2, va2, pr, ka1, va1, att_pk, wo,
    acc0, m0, acc1, m1, qa, doa, atb, dmix, dq, dqp, dkv, dkvp,
    rs_out, rs_sib, rs_mid, rs_z, pr_out, pr_in, lt, ltz,
    pan, pan_sib, pan_half, pan_z,
    s_far, r_far, s_fwd, r_fwd, s_pr, r_pr, s_w, r_w, s_att, r_att,
    s_rs, r_rs, s_rz, r_rz, s_pb, r_pb, s_l, r_l, s_lz, r_lz,
    s_a1, r_a1, s_a2, r_a2, s_a3, r_a3, s_a4, r_a4,
):
    ns, nh, ps, fs, hs, classes, piece = dims
    n, d = tiles.shape
    far, half = n // fs, n // ps
    sub_count = fs // ps
    z, h, p = lax.axis_index("seq"), lax.axis_index("head"), lax.axis_index("rep")

    def at_z(dz):
        return {"seq": lax.rem(z + dz, ns)}

    def at_x(e):
        place, bit = z, 1
        while bit < ns:
            if e & bit:
                place = place + bit - 2 * bit * lax.rem(lax.div(z, bit), 2)
            bit *= 2
        return {"seq": place}

    def at_p(dp):
        return {"rep": lax.rem(p + dp, ps)}

    def at_h(dh):
        return {"head": lax.rem(h + dh, nh)}

    sends = []

    def push(src, dst, ssem, rsem, where):
        copy = pltpu.make_async_remote_copy(
            src_ref=src, dst_ref=dst, send_sem=ssem, recv_sem=rsem,
            device_id=where, device_id_type=MESH,
        )
        copy.start()
        sends.append(copy)
        return copy

    barrier = pltpu.get_barrier_semaphore()
    peers = (
        [at_z(i) for i in range(1, ns)]
        + [at_p(i) for i in range(1, ps)]
        + [at_h(i) for i in range(1, nh)]
    )
    for peer in peers:
        pl.semaphore_signal(barrier, inc=1, device_id=peer, device_id_type=MESH)

    residues = [(c % sub_count) * ps + c // sub_count for c in range(fs)]
    count = counts[0]
    o1 = offsets[0, 0]
    o2 = offsets[0, 1]
    c2 = lax.rem(o2, ps) * sub_count + lax.div(o2, ps)

    def rows_of(c):
        return pl.ds(c * far, far)

    wqkv[pl.ds(0, hs), :] = w_query[...]
    wqkv[pl.ds(hs, hs), :] = jnp.zeros((hs, d), BF16)
    wqkv[pl.ds(2 * hs, hs), :] = w_key[...]
    wqkv[pl.ds(3 * hs, hs), :] = w_value[...]
    narrow = w_class[...].astype(F32)
    wcc[...] = jnp.concatenate([narrow, narrow], axis=0).astype(BF16)

    per = PERM // fs
    a = lax.broadcasted_iota(jnp.int32, (PERM, PERM), 0)
    b = lax.broadcasted_iota(jnp.int32, (PERM, PERM), 1)
    want = jnp.zeros((PERM, PERM), jnp.int32)
    for c in range(fs):
        want = jnp.where((a >= c * per) & (a < (c + 1) * per), (a - c * per) * fs + residues[c], want)
    perm = (want == b).astype(F32).astype(BF16)
    for blk in range(n // PERM):
        moved = nn(perm, tiles[pl.ds(blk * PERM, PERM), :]).astype(BF16)
        qkv = nt(moved, wqkv[...])
        q_part = (qkv[:, :128] * (1.0 / math.sqrt(hs))).astype(BF16)
        kv_part = qkv[:, 128:].astype(BF16)
        for c in range(fs):
            spot = pl.ds(c * far + blk * per, per)
            xt[spot, :] = moved[c * per:(c + 1) * per, :]
            qs[spot, :] = q_part[c * per:(c + 1) * per, :]
            kvs[spot, :] = kv_part[c * per:(c + 1) * per, :]

    def pick_far(ref):
        out = ref[rows_of(0), :].astype(F32)
        for c in range(1, fs):
            out = jnp.where(c2 == c, ref[rows_of(c), :].astype(F32), out)
        return out

    def pick_half(ref):
        out = ref[pl.ds(0, half), :].astype(F32)
        for c in range(1, ps):
            out = jnp.where(o1 == c, ref[pl.ds(c * half, half), :].astype(F32), out)
        return out

    high = lax.div(count, 256)
    tail = jnp.where(subs(TAIL) < 8, high.astype(F32), (count - high * 256).astype(F32)).astype(BF16)
    kv_all[0, 0, pl.ds(0, far), :] = pick_far(kvs).astype(BF16)
    kv_all[0, 0, pl.ds(far, TAIL), :] = tail
    pr[0, pl.ds(0, half), :] = pick_half(kvs).astype(BF16)
    pr[0, pl.ds(half, TAIL), :] = tail

    wo[:, pl.ds(0, hs), :] = jnp.zeros((nh, hs, d), BF16)
    wo[:, pl.ds(2 * hs, hs), :] = jnp.zeros((nh, hs, d), BF16)
    wo[0, pl.ds(hs, hs), :] = w_out[...]

    pl.semaphore_wait(barrier, len(peers))
    far_z = {}
    parts = (pl.ds(0, far // 2), pl.ds(far // 2, far // 2 + TAIL))

    def far_push(held, e, k, where):
        far_z[e, k] = push(
            kv_all.at[held, 0, parts[k], :], kv_all.at[e, 0, parts[k], :],
            s_far.at[e, k], r_far.at[e, k], where,
        )

    for e in list(range(2, ns, 2)) + [1]:
        for k in range(2):
            far_push(0, e, k, at_x(e))
    pr_c, fwd_c, w_c, att_c = {}, {}, {}, {}
    for dp in range(1, ps):
        pr_c[dp] = push(pr.at[0], pr.at[dp], s_pr.at[dp], r_pr.at[dp], at_p(dp))
        fwd_c[0, dp] = push(kv_all.at[0, 0], kv_all.at[0, dp], s_fwd.at[0, dp], r_fwd.at[0, dp], at_p(dp))
    for dh in range(1, nh):
        w_c[dh] = push(
            wo.at[0, pl.ds(hs, hs), :], wo.at[dh, pl.ds(hs, hs), :], s_w.at[dh], r_w.at[dh], at_h(dh)
        )

    def augment(kv, original, cnt):
        rows = kv.shape[0]
        lane = lanes(rows)
        kv = kv.astype(F32)
        bias = jnp.where(original.astype(F32) < cnt, 0.0, LOW)
        key = jnp.where(lane < hs, kv, jnp.where(lane == hs, bias, 1.0))
        value = jnp.where(lane < hs, 1.0, kv)
        return key.astype(BF16), value.astype(BF16)

    def remote_count(tail):
        tail = tail.astype(F32)
        return tail[0:1, 0:1] * 256.0 + tail[8:9, 0:1]

    def with_one(q):
        return jnp.where(lanes(q.shape[0]) == hs, 1.0, q.astype(F32)).astype(BF16)

    def forward(q, key, value):
        s = nt(q, key)
        top = jnp.max(s, axis=-1, keepdims=True)
        return top, nn(jnp.exp(s - top).astype(BF16), value)

    own_count = count.astype(F32)
    step = min(256, far // 2)
    for c in range(fs):
        key, value = augment(kvs[rows_of(c), :], subs(far) * fs + residues[c], own_count)
        ka0[rows_of(c), :] = key
        va0[rows_of(c), :] = value
    wide = min(256, n)
    for i in range(n // wide):
        spot = pl.ds(i * wide, wide)
        top, acc = forward(with_one(qs[spot, :]), ka0[...], va0[...])
        m0[spot, :] = jnp.broadcast_to(top, (wide, 128))
        acc0[spot, :] = acc
    for dp in range(ps):
        if dp:
            pr_c[dp].wait_recv()
        cnt = remote_count(pr[dp, pl.ds(half, TAIL), :])
        for k in range(sub_count):
            key, value = augment(pr[dp, pl.ds(k * far, far), :], subs(far) * fs + k * ps + o1, cnt)
            ka1[pl.ds(dp * half + k * far, far), :] = key
            va1[pl.ds(dp * half + k * far, far), :] = value
    q_half = with_one(pick_half(qs))
    wide = min(256, half)
    for i in range(half // wide):
        spot = pl.ds(i * wide, wide)
        top, acc = forward(q_half[i * wide:(i + 1) * wide, :], ka1[...], va1[...])
        m1[spot, :] = jnp.broadcast_to(top, (wide, 128))
        acc1[spot, :] = acc

    q_far = with_one(pick_far(qs))
    running = [None, None]

    def relay(e, k):
        far_z[e, k].wait_recv()
        far_push(e, e + 1, k, at_x(1))

    def share_far(e):
        for dp in range(1, ps):
            fwd_c[e, dp] = push(
                kv_all.at[e, 0], kv_all.at[e, dp], s_fwd.at[e, dp], r_fwd.at[e, dp], at_p(dp)
            )

    def arrived(e):
        for k in range(2):
            far_z[e, k].wait_recv()
        share_far(e)

    def use(e):
        for dp in range(ps):
            if dp:
                fwd_c[e, dp].wait_recv()
            key, value = augment(
                kv_all[e, dp, pl.ds(0, far), :], subs(far) * fs + o2,
                remote_count(kv_all[e, dp, pl.ds(far, TAIL), :]),
            )
            ka2[e * ps + dp] = key
            va2[e * ps + dp] = value
            top, acc = forward(q_far, key, value)
            if running[0] is not None:
                both = jnp.maximum(top, running[0])
                acc = running[1] * jnp.exp(running[0] - both) + acc * jnp.exp(top - both)
                top = both
            running[:] = [top, acc]

    for e in range(2, ns, 2):
        relay(e, 0)
        if e == 2:
            use(0)
        relay(e, 1)
        share_far(e)
        arrived(e - 1)
        use(e - 1)
        use(e)
    arrived(ns - 1)
    use(ns - 1)
    top2, acc2 = running

    for c in range(fs):
        rows = rows_of(c)
        in_half = pl.ds((c % sub_count) * far, far)
        t0 = m0[rows, 0:1]
        t1 = jnp.where(o1 == c // sub_count, m1[in_half, 0:1], LOW)
        t2 = jnp.where(c2 == c, top2, LOW)
        top = jnp.maximum(t0, jnp.maximum(t1, t2))
        acc = acc0[rows, :] * jnp.exp(t0 - top) + acc1[in_half, :] * jnp.exp(t1 - top) + acc2 * jnp.exp(t2 - top)
        total = acc[:, 0:1]
        lane = lanes(far)
        att = jnp.where(lane < hs, 0.0, acc / total)
        atb[rows, :] = att.astype(BF16)
        one, two, rest = three(-(top + jnp.log(total)))
        aux = jnp.where(lane == hs, 1.0, jnp.where(lane == hs + 1, one, jnp.where(lane == hs + 2, two, jnp.where(lane == hs + 3, rest, 0.0))))
        qa[rows, :] = jnp.where(lane < hs, qs[rows, :].astype(F32), aux).astype(BF16)
        both = pltpu.roll(att, hs, 1)[far // 2:, :] + att[:far // 2, :]
        att_pk[0, c] = both.astype(BF16)
        for dh in range(1, nh):
            att_c[c, dh] = push(att_pk.at[0, c], att_pk.at[dh, c], s_att.at[c, dh], r_att.at[c, dh], at_h(dh))
    for dh in range(1, nh):
        w_c[dh].wait_recv()

    loss = jnp.zeros((1, 1), F32)
    g = gain[...].reshape(1, d)
    span = step * fs
    marks = labels[...].reshape(1, n).astype(F32)
    pick_row = lax.broadcasted_iota(jnp.int32, (step, span), 0) * fs
    pick_col = lax.broadcasted_iota(jnp.int32, (step, span), 1)
    for i in range(n // step):
        start = i * step
        c, inner = start // far, start % far
        rows = pl.ds(start, step)
        mixed = xt[rows, :].astype(F32)
        for dh in range(nh):
            if dh and inner == 0:
                att_c[c, dh].wait_recv()
            if inner < far // 2:
                term = nn(att_pk[dh, c, pl.ds(inner, step), :], wo[dh, pl.ds(0, 2 * hs), :])
            else:
                term = nn(att_pk[dh, c, pl.ds(inner - far // 2, step), :], wo[dh, pl.ds(hs, 2 * hs), :])
            mixed = mixed + term.astype(BF16).astype(F32)
        center = mixed - jnp.mean(mixed, axis=-1, keepdims=True)
        inv_dev = lax.rsqrt(jnp.mean(center * center, axis=-1, keepdims=True) + 1e-05)
        normal = center * inv_dev
        normed = (normal * g).astype(BF16)
        logits = nt(wcc[...], normed)[:classes, :]
        peak = jnp.max(logits, axis=0, keepdims=True)
        log_total = jnp.log(jnp.sum(jnp.exp(logits - peak), axis=0, keepdims=True)) + peak
        kind = lax.broadcasted_iota(jnp.int32, (classes, step), 0).astype(F32)
        chosen = (pick_row + residues[c] == pick_col).astype(F32).astype(BF16)
        block = jnp.broadcast_to(marks[:, inner * fs:inner * fs + span], (classes, span)).astype(BF16)
        onehot = (kind == nt(block, chosen)).astype(F32)
        spot = lax.broadcasted_iota(jnp.int32, (1, step), 1)
        ok = ((spot + inner) * fs + residues[c] < count).astype(F32)
        cross = log_total - jnp.sum(onehot * logits, axis=0, keepdims=True)
        loss = loss + jnp.sum(ok * cross, axis=1, keepdims=True)
        d_logits = (jnp.exp(logits - log_total) - onehot) * ok * (1.0 / n)
        hi = d_logits.astype(BF16).astype(F32)
        split = jnp.concatenate([hi, d_logits - hi], axis=0).astype(BF16)
        d_normal = tn(split, wcc[...]) * g
        d_mixed = inv_dev * (
            d_normal
            - jnp.mean(d_normal, axis=-1, keepdims=True)
            - normal * jnp.mean(d_normal * normal, axis=-1, keepdims=True)
        )
        d_mixed = d_mixed.astype(BF16)
        dmix[rows, :] = d_mixed
        d_att = nt(d_mixed, wo[0, pl.ds(0, 2 * hs), :]).astype(BF16).astype(F32)
        delta = jnp.sum(d_att * atb[rows, :].astype(F32), axis=-1, keepdims=True)
        one, two, rest = three(-delta)
        lane = lanes(step)
        aux = jnp.where(lane == 0, one, jnp.where(lane == 1, two, jnp.where(lane == 2, rest, d_att)))
        doa[rows, :] = aux.astype(BF16)
    lt[0, :, :] = jnp.broadcast_to(loss * (1.0 / n), (8, 128))
    lt_c = {dp: push(lt.at[0], lt.at[dp], s_l.at[dp], r_l.at[dp], at_p(dp)) for dp in range(1, ps)}

    def backward(q, do, key, value):
        prob = jnp.exp(nt(key, q))
        d_score = (prob * nt(value, do)).astype(BF16)
        d_key = nn(d_score, q)
        d_value = nn(prob.astype(BF16), do)
        return tn(d_score, key), jnp.where(lanes(key.shape[0]) < hs, d_key, d_value)

    q_far = pick_far(qa).astype(BF16)
    do_far = pick_far(doa).astype(BF16)
    dq_far = None
    rz_c, rs_c, own = {}, {}, {}

    def settle(e):
        total = own[e]
        for dp in range(1, ps):
            rs_c[e, dp].wait_recv()
            total = total + rs_sib[e, dp].astype(F32)
        own[e] = total
        if e % 2:
            rs_mid[e] = total.astype(BF16)
            rz_c[e] = push(rs_mid.at[e], rs_z.at[e], s_rz.at[e], r_rz.at[e], at_x(1))

    turns = list(range(3, ns, 2)) + list(range(2, ns, 2)) + [1, 0]
    for turn, e in enumerate(turns):
        for dp in list(range(1, ps)) + [0]:
            if dp == 0 and turn:
                settle(turns[turn - 1])
            key_rows = e * ps + dp
            d_q, d_kv = backward(q_far, do_far, ka2[key_rows], va2[key_rows])
            dq_far = d_q if dq_far is None else dq_far + d_q
            if dp:
                rs_out[e, dp] = d_kv.astype(BF16)
                rs_c[e, dp] = push(
                    rs_out.at[e, dp], rs_sib.at[e, dp], s_rs.at[e, dp], r_rs.at[e, dp], at_p(ps - dp)
                )
            else:
                own[e] = d_kv
    whole_loss = lt[0, :, :]
    for dp in range(1, ps):
        lt_c[dp].wait_recv()
        whole_loss = whole_loss + lt[dp, :, :]
    ltz[0, :, :] = whole_loss
    lz_c = {dz: push(ltz.at[0], ltz.at[dz], s_lz.at[dz], r_lz.at[dz], at_z(dz)) for dz in range(1, ns)}

    q_half = pick_half(qa).astype(BF16)
    do_half = pick_half(doa).astype(BF16)
    pb_c = {}
    dq_half = None
    for dp in list(range(1, ps)) + [0]:
        key_rows = pl.ds(dp * half, half)
        d_q, d_kv = backward(q_half, do_half, ka1[key_rows, :], va1[key_rows, :])
        dq_half = d_q if dq_half is None else dq_half + d_q
        if dp:
            pr_out[dp] = d_kv.astype(BF16)
            pb_c[dp] = push(pr_out.at[dp], pr_in.at[dp], s_pb.at[dp], r_pb.at[dp], at_p(ps - dp))
        else:
            dkvp[...] = d_kv
    dqp[...] = dq_half

    for e in range(2, ns, 2):
        rz_c[e + 1].wait_recv()
        rs_mid[e] = (own[e] + rs_z[e + 1].astype(F32)).astype(BF16)
        rz_c[e] = push(rs_mid.at[e], rs_z.at[e], s_rz.at[e], r_rz.at[e], at_x(e))

    tile = min(512, n)
    for j in range(n // tile):
        key_rows = pl.ds(j * tile, tile)
        total = None
        for i in range(n // tile):
            rows = pl.ds(i * tile, tile)
            d_q, d_kv = backward(qa[rows, :], doa[rows, :], ka0[key_rows, :], va0[key_rows, :])
            total = d_kv if total is None else total + d_kv
            if j:
                dq[rows, :] += d_q
            else:
                dq[rows, :] = d_q
        dkv[key_rows, :] = total

    for c in range(fs):
        rows = rows_of(c)
        in_half = pl.ds((c % sub_count) * far, far)
        part = dq[rows, :]
        part = part + jnp.where(o1 == c // sub_count, dqp[in_half, :], 0.0)
        part = part + jnp.where(c2 == c, dq_far, 0.0)
        qa[rows, :] = jnp.where(lanes(far) < hs, part * (1.0 / math.sqrt(hs)), 0.0).astype(BF16)

    quarter = ns * piece
    first, second, third, fourth = {}, {}, {}, {}

    def start_panel(k, panel):
        for j in range(d // 128):
            pan[k, pl.ds(j * 128, 128), :] = panel[:, j * 128:(j + 1) * 128].astype(BF16)
        if quarter * ps > d:
            pan[k, pl.ds(d, quarter * ps - d), :] = jnp.zeros((quarter * ps - d, 128), BF16)
        for dp in range(1, ps):
            there = pl.multiple_of(lax.rem(p + dp, ps) * quarter, 16)
            first[k, dp] = push(
                pan.at[k, pl.ds(there, quarter), :], pan_sib.at[k, dp],
                s_a1.at[k, dp], r_a1.at[k, dp], at_p(dp),
            )

    def second_panel(k):
        here = pl.multiple_of(p * quarter, 16)
        total = pan[k, pl.ds(here, quarter), :].astype(F32)
        for dp in range(1, ps):
            first[k, dp].wait_recv()
            total = total + pan_sib[k, dp].astype(F32)
        pan_half[k] = total.astype(BF16)
        for dz in range(1, ns):
            there = pl.multiple_of(lax.rem(z + dz, ns) * piece, 16)
            second[k, dz] = push(
                pan_half.at[k, pl.ds(there, piece), :], pan_z.at[k, dz],
                s_a2.at[k, dz], r_a2.at[k, dz], at_z(dz),
            )

    def third_panel(k):
        here = pl.multiple_of(z * piece, 16)
        total = pan_half[k, pl.ds(here, piece), :].astype(F32)
        for dz in range(1, ns):
            second[k, dz].wait_recv()
            total = total + pan_z[k, dz].astype(F32)
        spot = pl.ds(pl.multiple_of(p * quarter + z * piece, 16), piece)
        res[k, spot, :] = total.astype(BF16)
        for dz in range(1, ns):
            third[k, dz] = push(
                res.at[k, spot, :], res.at[k, spot, :], s_a3.at[k, dz], r_a3.at[k, dz], at_z(dz)
            )
        share(k, 0)

    def share(k, dz):
        spot = pl.ds(pl.multiple_of(p * quarter + lax.rem(z + ns - dz, ns) * piece, 16), piece)
        for dp in range(1, ps):
            fourth[k, dz, dp] = push(
                res.at[k, spot, :], res.at[k, spot, :], s_a4.at[k, dz, dp], r_a4.at[k, dz, dp], at_p(dp)
            )

    def fourth_panel(k):
        for dz in range(1, ns):
            third[k, dz].wait_recv()
            share(k, dz)

    start_panel(0, tn(qa[...], xt[...]) + tn(atb[...], dmix[...]))

    half_sum = dkvp[...]
    for dp in range(1, ps):
        pb_c[dp].wait_recv()
        half_sum = half_sum + pr_in[dp].astype(F32)
    dkvp[...] = half_sum
    second_panel(0)
    for c in range(fs):
        rows = rows_of(c)
        in_half = pl.ds((c % sub_count) * far, far)
        part = dkv[rows, :] + jnp.where(o1 == c // sub_count, dkvp[in_half, :], 0.0)
        dkv[rows, :] = part
        doa[rows, :] = jnp.where(c2 == c, 0.0, part).astype(BF16)
    near = tn(doa[...], xt[...])
    xt_far = pick_far(xt).astype(BF16)
    settle(0)
    own_far = own[0] + pick_far(dkv)
    for e in [1] + list(range(2, ns, 2)):
        rz_c[e].wait_recv()
        own_far = own_far + rs_z[e].astype(F32)
    start_panel(1, near + tn(own_far.astype(BF16), xt_far))
    third_panel(0)
    second_panel(1)
    fourth_panel(0)
    third_panel(1)
    total = ltz[0, :, :]
    for dz in range(1, ns):
        lz_c[dz].wait_recv()
        total = total + ltz[dz, :, :]
    loss_out[...] = total
    fourth_panel(1)
    for k in range(2):
        for dz in range(ns):
            for dp in range(1, ps):
                fourth[k, dz, dp].wait_recv()
    for copy in sends:
        copy.wait_send()


def unpack(hs, res, loss, tile_loss, g_query, g_key, g_value, g_out):
    tile_loss[0] = loss[0, 0]
    for j in range(g_query.shape[1] // 128):
        cols = pl.ds(j * 128, 128)
        g_query[:, cols] = res[0, pl.ds(j * 128, hs), :].astype(F32)
        g_out[:, cols] = res[0, pl.ds(j * 128 + hs, hs), :].astype(F32)
        g_key[:, cols] = res[1, pl.ds(j * 128, hs), :].astype(F32)
        g_value[:, cols] = res[1, pl.ds(j * 128 + hs, hs), :].astype(F32)


def body(ns, nh, ps, tiles, labels, counts, offsets, w_query, w_key, w_value, w_out, ln_gain, w_class):
    n, d = tiles.shape
    hs = w_query.shape[1]
    classes = w_class.shape[1]
    shards = ns * ps
    fs = shards // 4
    far, half = n // fs, n // ps
    piece = -(-d // (shards * 16)) * 16
    quarter = ns * piece
    vmem = pltpu.VMEM
    dma = lambda *shape: pltpu.SemaphoreType.DMA(shape)
    scratch = [
        vmem((4 * hs, d), BF16), vmem((2 * classes, d), BF16),
        vmem((n, d), BF16), vmem((n, 128), BF16), vmem((n, 128), BF16),
        vmem((n, 128), BF16), vmem((n, 128), BF16),
        vmem((ns, ps, far + TAIL, 128), BF16),
        vmem((shards, far, 128), BF16), vmem((shards, far, 128), BF16),
        vmem((ps, half + TAIL, 128), BF16), vmem((n, 128), BF16), vmem((n, 128), BF16),
        vmem((nh, fs, far // 2, 128), BF16), vmem((nh, 3 * hs, d), BF16),
        vmem((n, 128), F32), vmem((n, 128), F32), vmem((half, 128), F32), vmem((half, 128), F32),
        vmem((n, 128), BF16), vmem((n, 128), BF16), vmem((n, 128), BF16), vmem((n, d), BF16),
        vmem((n, 128), F32), vmem((half, 128), F32), vmem((n, 128), F32), vmem((half, 128), F32),
        vmem((ns, ps, far, 128), BF16), vmem((ns, ps, far, 128), BF16),
        vmem((ns, far, 128), BF16), vmem((ns, far, 128), BF16),
        vmem((ps, half, 128), BF16), vmem((ps, half, 128), BF16),
        vmem((ps, 8, 128), F32), vmem((ns, 8, 128), F32),
        vmem((2, ps * quarter, 128), BF16), vmem((2, ps, quarter, 128), BF16),
        vmem((2, quarter, 128), BF16), vmem((2, ns, piece, 128), BF16),
        dma(ns, 2), dma(ns, 2), dma(ns, ps), dma(ns, ps), dma(ps), dma(ps), dma(nh), dma(nh), dma(fs, nh), dma(fs, nh),
        dma(ns, ps), dma(ns, ps), dma(ns), dma(ns), dma(ps), dma(ps), dma(ps), dma(ps), dma(ns), dma(ns),
        dma(2, ps), dma(2, ps), dma(2, ns), dma(2, ns), dma(2, ns), dma(2, ns), dma(2, ns, ps), dma(2, ns, ps),
    ]
    whole = pl.BlockSpec(memory_space=pltpu.VMEM)
    scalar = pl.BlockSpec(memory_space=pltpu.SMEM)
    res, loss = pl.pallas_call(
        functools.partial(kernel, (ns, nh, ps, fs, hs, classes, piece)),
        out_shape=(
            jax.ShapeDtypeStruct((2, ps * quarter, 128), BF16),
            jax.ShapeDtypeStruct((8, 128), F32),
        ),
        in_specs=[whole, whole, scalar, scalar] + [whole] * 6,
        out_specs=(whole, whole),
        scratch_shapes=scratch,
        compiler_params=pltpu.CompilerParams(
            collective_id=0, has_side_effects=True, vmem_limit_bytes=56 * 1024 * 1024
        ),
    )(tiles, labels, counts, offsets.T, w_query.T, w_key.T, w_value.T, w_out, ln_gain, w_class.T)
    flat = jax.ShapeDtypeStruct((hs, d), F32)
    tile_loss, g_query, g_key, g_value, g_out = pl.pallas_call(
        functools.partial(unpack, hs),
        out_shape=(jax.ShapeDtypeStruct((1,), F32), flat, flat, flat, flat),
        in_specs=[whole, whole],
        out_specs=(scalar, whole, whole, whole, whole),
    )(res, loss)
    return (tile_loss, g_query.T, g_key.T, g_value.T, g_out)


def solution(mesh):
    placed = (
        P(("slide", "seq", "rep"), None),
        P(("slide", "seq", "rep")),
        P(("slide", "seq", "rep")),
        P(None, "head"),
        P(None, "head"),
        P(None, "head"),
        P(None, "head"),
        P("head", None),
        P(),
        P(),
    )
    sizes = mesh.shape
    return jax.shard_map(
        functools.partial(body, sizes["seq"], sizes["head"], sizes["rep"]),
        mesh=mesh,
        in_specs=placed,
        out_specs=(
            P("slide"),
            P("slide", "head"),
            P("slide", "head"),
            P("slide", "head"),
            P("head", "slide"),
        ),
        check_vma=False,
    )
```
